256 devices in a mesh: ctx: 32 (over x, z), tp: 8 (over y, core).
Axes of the slice: x: 4, y: 4, z: 8, core: 2. Of those that a mesh axis runs over, the one named last changes fastest.
Arguments:
- query: bfloat16 [16384, 8192], P('ctx', 'tp'), may hold values from -2 to 2
- key_in: bfloat16 [16384, 8192], P('ctx', 'tp'), may hold values from -2 to 2
- value: bfloat16 [16384, 8192], P('ctx', 'tp'), may hold values from -6 to 6
- gate: bfloat16 [16384, 8192], P('ctx', 'tp'), may hold values from -6 to 6
- gain: float32 [8192], P('tp'), may hold values from 0.25 to 1.75
- grad_out: bfloat16 [16384, 8192], P('ctx', 'tp'), may hold values from -6 to 6
Outputs:
- gated: bfloat16 [16384, 8192], P('ctx', 'tp')
- grad_query: bfloat16 [16384, 8192], P('ctx', 'tp')
- grad_key: bfloat16 [16384, 8192], P('ctx', 'tp')
- grad_value: bfloat16 [16384, 8192], P('ctx', 'tp')
- grad_gate: bfloat16 [16384, 8192], P('ctx', 'tp')
- gain_gradient: float32 [8192], P('tp')
The draws below stay inside these ranges and needn't reach their ends.
All inputs are finite; a program needn't handle non-finite values.
Results may differ from the reference program's by a relative error of at most 0.0058.
Values sent between devices are 32-bit elements; how exact they have to be, the bound alone decides.
A program may use at most 128 MiB of HBM per device.

```python
import jax
import jax.numpy as jnp
from jax import lax

ATTENTION_HEADS = 64
HEAD_WIDTH = 128
TOK_DEV = 512
SEQ = 16384
FEAT = 8192
N_CTX = 32


def level_of(own_key, dims, cuts, low, high):
    loudness, own = 1.0, jax.random.fold_in(own_key, 6)
    for axis_at, shards_of in cuts:
        heights = jnp.exp(jax.random.uniform(jax.random.fold_in(own, axis_at), (shards_of,), jnp.float32, low / len(cuts), high / len(cuts)))
        loudness = loudness * jnp.repeat(heights, dims[axis_at] // shards_of).reshape([-1 if axis == axis_at else 1 for axis in range(len(dims))])
    return loudness


def gaussian(rng, shape, scale, most, pieces=(), held_as=jnp.bfloat16):
    factor_of = level_of(rng, shape, pieces, -0.22, 0.18) if pieces else 1.0
    result = jax.random.normal(rng, shape, jnp.float32) * scale * factor_of
    return jnp.minimum(jnp.maximum(result, -most), most).astype(held_as)


def setup_inputs(seed: int = 0) -> dict:
    splits = jax.random.split(jax.random.key(seed), 7)
    return {
        "query": gaussian(splits[0], (SEQ, FEAT), 0.3, 2.0, ((0, 32), (1, 8))),
        "key_in": gaussian(splits[1], (SEQ, FEAT), 0.3, 2.0, ((0, 32), (1, 8))),
        "value": gaussian(splits[2], (SEQ, FEAT), 1.0, 6.0, ((0, 32), (1, 8))),
        "gate": gaussian(splits[3], (SEQ, FEAT), 1.0, 6.0, ((0, 32), (1, 8))),
        "gain": jnp.clip(1.0 + 0.15 * jax.random.normal(splits[4], (FEAT,), jnp.float32), 0.25, 1.75),
        "grad_out": gaussian(splits[5], (SEQ, FEAT), 1.0, 6.0, ((0, 32), (1, 8))),
    }


def split_heads(x):
    return x.reshape(N_CTX, TOK_DEV, ATTENTION_HEADS, HEAD_WIDTH).transpose(2, 0, 1, 3)

def join_heads(x):
    return x.transpose(1, 2, 0, 3).reshape(N_CTX * TOK_DEV, ATTENTION_HEADS * HEAD_WIDTH)

def causal_mask():
    rows = jnp.arange(TOK_DEV)
    return rows[:, None] >= rows[None, :]

def block_probs(qf, kf):
    scores = jnp.einsum('ctd,csd->cts', qf, kf)
    return jnp.where(causal_mask()[None], scores, 0.0).astype(jnp.bfloat16)

def forward_head(inputs):
    qh, kh, vh = inputs
    qf = qh.astype(jnp.float32)
    kf = kh.astype(jnp.float32)
    vf = vh.astype(jnp.float32)
    local = jnp.einsum('ctd,cte->cde', kf, vf)
    running = jnp.cumsum(local, axis=0)
    prefix = jnp.concatenate([jnp.zeros((1, HEAD_WIDTH, HEAD_WIDTH), jnp.float32), running[:-1]], axis=0)
    prefix_b = prefix.astype(jnp.bfloat16)
    probs = block_probs(qf, kf)
    attention_output = jnp.einsum('cts,cse->cte', probs.astype(jnp.float32), vf)
    attention_output = attention_output + jnp.einsum('ctd,cde->cte', qf, prefix_b.astype(jnp.float32))
    return (attention_output, prefix_b)

def backward_head(inputs):
    qh, kh, vh, doh, prefix_b = inputs
    qf = qh.astype(jnp.float32)
    kf = kh.astype(jnp.float32)
    vf = vh.astype(jnp.float32)
    dof = doh.astype(jnp.float32)
    pf = prefix_b.astype(jnp.float32)
    probs = block_probs(qf, kf).astype(jnp.float32)
    gstate = jnp.einsum('ctd,cte->cde', qf, dof)
    later = jnp.cumsum(gstate[::-1], axis=0)[::-1]
    suffix = jnp.concatenate([later[1:], jnp.zeros((1, HEAD_WIDTH, HEAD_WIDTH), jnp.float32)], axis=0)
    sf = suffix.astype(jnp.bfloat16).astype(jnp.float32)
    dscores = jnp.einsum('cte,cse->cts', dof, vf)
    dprobs = jnp.where(causal_mask()[None], dscores, 0.0).astype(jnp.bfloat16).astype(jnp.float32)
    dq = jnp.einsum('cts,csd->ctd', dprobs, kf) + jnp.einsum('cte,cde->ctd', dof, pf)
    dk = jnp.einsum('cts,ctd->csd', dprobs, qf) + jnp.einsum('cse,cde->csd', vf, sf)
    dv = jnp.einsum('cts,cte->cse', probs, dof) + jnp.einsum('csd,cde->cse', kf, sf)
    return (dq.astype(jnp.bfloat16), dk.astype(jnp.bfloat16), dv.astype(jnp.bfloat16))

def reference(query, key_in, value, gate, gain, grad_out):
    qh = split_heads(query)
    kh = split_heads(key_in)
    vh = split_heads(value)
    attn_h, prefix_b = lax.map(forward_head, (qh, kh, vh))
    attention_output = join_heads(attn_h)
    mean_sq = lax.optimization_barrier(jnp.sum(attention_output * attention_output, axis=1, keepdims=True)) / (ATTENTION_HEADS * HEAD_WIDTH)
    inverse_root = lax.rsqrt(mean_sq + 1e-06)
    scaled_input = attention_output * inverse_root
    normalized_output = scaled_input * gain[None, :]
    sg = jax.nn.sigmoid(gate.astype(jnp.float32))
    gated = (normalized_output * sg).astype(jnp.bfloat16)
    cot = grad_out.astype(jnp.float32)
    grad_gate = (cot * normalized_output * sg * (1.0 - sg)).astype(jnp.bfloat16)
    normalized_gradient = cot * sg
    gain_gradient = lax.optimization_barrier(jnp.sum(normalized_gradient * scaled_input, axis=0))
    centered_gradient = normalized_gradient * gain[None, :]
    product_mean = lax.optimization_barrier(jnp.sum(centered_gradient * scaled_input, axis=1, keepdims=True)) / (ATTENTION_HEADS * HEAD_WIDTH)
    attention_gradient = (inverse_root * (centered_gradient - scaled_input * product_mean)).astype(jnp.bfloat16)
    dq, dk, dv = lax.map(backward_head, (qh, kh, vh, split_heads(attention_gradient), prefix_b))
    return (gated, join_heads(dq), join_heads(dk), join_heads(dv), grad_gate, gain_gradient)
```

```python
import functools

import jax
import jax.numpy as jnp
from jax import lax
from jax.experimental import pallas as pl
from jax.experimental.pallas import tpu as pltpu
from jax.sharding import PartitionSpec as P

HEADS = 64
WIDTH = 128
MESH = pl.DeviceIdType.MESH
F32 = jnp.float32
BF16 = jnp.bfloat16
NX, NZ = 4, 8
CTX = NX * NZ
TP = 8
TOK = 512
HD = 8
FEAT_DEV = HD * WIDTH
HALVES = 2
HH = HD // HALVES
PIECE = HH * WIDTH // CTX
HALF_TOK = TOK // 2
STEPS_Z = (4, 3, -3, 2, -2, 1, -1, 0)


def dot(a, b, ca, cb):
    return lax.dot_general(a, b, (((ca,), (cb,)), ((), ())), preferred_element_type=F32)


def kernel(
    q_in, k_in, v_in, g_in, c_in, gain_ref,
    gated_out, dq_out, dk_out, dv_out, gg_out, gain_out,
    q, k, v, g, c,
    sg, w, attn, dk, dv, probs, d, pb,
    o_gated, o_dq, o_dk, o_dv, o_gg,
    l_a, r_a, p_a, s_a, l_b, r_b, p_b, s_b,
    acc_s, acc_p, rinv_c, pm_c, st, st_r, gs, gx_r, gz, gz_r,
    in_sem, out_sem,
    a_s1, a_r1, a_s2, a_r2, b_s1, b_r1, b_s2, b_r2,
    t_s, t_r, x_s, x_r, z_s, z_r,
):
    me = lax.axis_index("ctx")
    tp = lax.axis_index("tp")
    x, z = me // NZ, lax.rem(me, NZ)

    half_cols = HH * WIDTH

    def load(src, dst, sem, half):
        cols = pl.ds(half * half_cols, half_cols)
        return pltpu.make_async_copy(src.at[:, cols], dst.at[:, cols], in_sem.at[sem, half])

    pairs = ((k_in, k, 0), (v_in, v, 1), (q_in, q, 2), (g_in, g, 3), (c_in, c, 4))
    for half in range(HALVES):
        for src, dst, sem in pairs[:2]:
            load(src, dst, sem, half).start()
    for half in range(HALVES):
        for src, dst, sem in pairs[2:]:
            load(src, dst, sem, half).start()

    barrier = pltpu.get_barrier_semaphore()

    @pl.loop(1, CTX)
    def _(i):
        pl.semaphore_signal(barrier, inc=1, device_id=(lax.rem(me + i, CTX), tp), device_id_type=MESH)

    @pl.loop(1, TP)
    def _(i):
        pl.semaphore_signal(barrier, inc=1, device_id=(me, lax.rem(tp + i, TP)), device_id_type=MESH)

    def to_all(start):
        @pl.loop(0, NX)
        def _(a):
            for b, dz in enumerate(STEPS_Z):
                dx = lax.rem(2 + 3 * (a + b), NX)
                to = lax.rem(x + dx, NX) * NZ + lax.rem(z + dz + NZ, NZ)
                if dz == 0:
                    @pl.when(dx != 0)
                    def _():
                        start(to)
                else:
                    start(to)

    def remote(src, dst, ss, rs, to):
        return pltpu.make_async_remote_copy(
            src_ref=src, dst_ref=dst, send_sem=ss, recv_sem=rs, device_id=to, device_id_type=MESH
        )

    def others(buf, ss, rs):
        part = buf.at[pl.ds(0, CTX - 1)]
        return remote(part, part, ss, rs, (lax.rem(me + 1, CTX), tp))

    def send_states(half, l, r, ss, rs):
        base = half * HH * WIDTH

        def rows(j):
            return pl.ds(pl.multiple_of(base + j * PIECE, PIECE), PIECE)

        to_all(lambda j: remote(l.at[rows(j)], r.at[half, me], ss.at[half], rs.at[half], (j, tp)).start())
        r[half, me] = l[rows(me), :]

    def add_up(half, reverse, r, p, s, s1, r1, s2, r2):
        others(r.at[half], s1.at[half], r1.at[half]).wait_recv()
        total = jnp.zeros((PIECE, WIDTH), F32)
        for j in (range(CTX - 1, -1, -1) if reverse else range(CTX)):
            p[half, j] = total
            total = total + r[half, j]
        to_all(lambda j: remote(p.at[half, j], s.at[half, me], s2.at[half], r2.at[half], (j, tp)).start())
        s[half, me] = p[half, me]

    def arrived(half, s, s2, r2):
        others(s.at[half], s2.at[half], r2.at[half]).wait_recv()

    def state_of(s, half, i):
        return s[half, pl.ds(pl.multiple_of(i * (WIDTH // PIECE), WIDTH // PIECE), WIDTH // PIECE)].reshape(WIDTH, WIDTH)

    def cols_of(h):
        return pl.ds(pl.multiple_of(h * WIDTH, WIDTH), WIDTH)

    for half in range(HALVES):
        for src, dst, sem in pairs[:2]:
            load(src, dst, sem, half).wait()

        @pl.loop(half * HH, (half + 1) * HH)
        def _(h):
            cols = cols_of(h)
            l_a[cols, :] = dot(k[:, cols], v[:, cols], 0, 0)

        if half == 0:
            pl.semaphore_wait(barrier, CTX - 1 + TP - 1)
        send_states(half, l_a, r_a, a_s1, a_r1)

    lower = lax.broadcasted_iota(jnp.int32, (HALF_TOK, HALF_TOK), 0) >= lax.broadcasted_iota(
        jnp.int32, (HALF_TOK, HALF_TOK), 1
    )
    lo, hi = pl.ds(0, HALF_TOK), pl.ds(HALF_TOK, HALF_TOK)

    acc_s[...] = jnp.zeros_like(acc_s)
    acc_p[...] = jnp.zeros_like(acc_p)

    for half in range(HALVES):
        for src, dst, sem in pairs[2:]:
            load(src, dst, sem, half).wait()

        @pl.loop(half * HH, (half + 1) * HH)
        def _(h):
            cols = cols_of(h)
            q0, q1 = q[lo, cols], q[hi, cols]
            k0, k1 = k[lo, cols], k[hi, cols]
            v0, v1 = v[lo, cols], v[hi, cols]
            p00 = jnp.where(lower, dot(q0, k0, 1, 1), 0.0).astype(BF16)
            p10 = dot(q1, k0, 1, 1).astype(BF16)
            p11 = jnp.where(lower, dot(q1, k1, 1, 1), 0.0).astype(BF16)
            probs[h, 0] = p00
            probs[h, 1] = p10
            probs[h, 2] = p11
            attn[lo, cols] = dot(p00, v0, 1, 0)
            attn[hi, cols] = dot(p10, v0, 1, 0) + dot(p11, v1, 1, 0)
            gain = gain_ref[pl.ds(h, 1), :]
            for t in range(4):
                rows = pl.ds(t * 128, 128)
                gate = jax.nn.sigmoid(g[rows, cols].astype(F32))
                sg[rows, cols] = gate
                w[rows, cols] = c[rows, cols].astype(F32) * gate * gain

        add_up(half, False, r_a, p_a, s_a, a_s1, a_r1, a_s2, a_r2)

    for half in range(HALVES):
        arrived(half, s_a, a_s2, a_r2)

        @pl.loop(0, HH)
        def _(i):
            h = half * HH + i
            cols = cols_of(h)
            prefix = state_of(s_a, half, i).astype(BF16)
            pb[h] = prefix
            for t in range(4):
                rows = pl.ds(t * 128, 128)
                a = attn[rows, cols] + dot(q[rows, cols], prefix, 1, 0)
                attn[rows, cols] = a
                acc_s[rows, :] += a * a
                acc_p[rows, :] += a * w[rows, cols]

    for t in range(4):
        rows = pl.ds(t * 128, 128)
        st[pl.ds(t, 1), :] = jnp.sum(acc_s[rows, :].T, axis=0, keepdims=True)
        st[pl.ds(4 + t, 1), :] = jnp.sum(acc_p[rows, :].T, axis=0, keepdims=True)

    @pl.loop(1, TP)
    def _(i):
        remote(st, st_r.at[tp], t_s.at[0], t_r.at[0], (me, lax.rem(tp + i, TP))).start()

    st_r[tp] = st[...]
    peers = st_r.at[pl.ds(0, TP - 1)]
    peers_copy = remote(peers, peers, t_s.at[0], t_r.at[0], (me, lax.rem(tp + 1, TP)))
    peers_copy.wait_recv()
    sums = jnp.sum(st_r[...], axis=0)
    feat = float(HEADS * WIDTH)
    rinv = lax.rsqrt(sums[0:4] / feat + 1e-06)
    mean = sums[4:8] * rinv / feat
    for t in range(4):
        rows = pl.ds(t * 128, 128)
        rinv_c[rows, :] = jnp.broadcast_to(rinv[t : t + 1], (128, 128)).T
        pm_c[rows, :] = jnp.broadcast_to(mean[t : t + 1], (128, 128)).T

    for half in range(HALVES):
        @pl.loop(half * HH, (half + 1) * HH)
        def _(h):
            cols = cols_of(h)
            for t in range(4):
                rows = pl.ds(t * 128, 128)
                ri = rinv_c[rows, :]
                xhat = attn[rows, cols] * ri
                d[rows, cols] = (ri * (w[rows, cols] - xhat * pm_c[rows, :])).astype(BF16)
            l_b[cols, :] = dot(q[:, cols], d[:, cols], 0, 0)

        send_states(half, l_b, r_b, b_s1, b_r1)

    def put(src, dst, sem, half):
        cols = pl.ds(half * half_cols, half_cols)
        return pltpu.make_async_copy(src.at[:, cols], dst.at[:, cols], out_sem.at[sem, half])

    for half in range(HALVES):
        @pl.loop(half * HH, (half + 1) * HH)
        def _(h):
            cols = cols_of(h)
            gain = gain_ref[pl.ds(h, 1), :]
            part = jnp.zeros((8, WIDTH), F32)
            for t in range(4):
                rows = pl.ds(t * 128, 128)
                xhat = attn[rows, cols] * rinv_c[rows, :]
                normed = xhat * gain
                gate = sg[rows, cols]
                cot = c[rows, cols].astype(F32)
                o_gated[rows, cols] = (normed * gate).astype(BF16)
                o_gg[rows, cols] = (cot * normed * gate * (1.0 - gate)).astype(BF16)
                part = part + jnp.sum((cot * gate * xhat).reshape(16, 8, WIDTH), axis=0)
            gs[pl.ds(h, 1), :] = jnp.sum(part, axis=0, keepdims=True)

            q0, q1 = q[lo, cols], q[hi, cols]
            k0, k1 = k[lo, cols], k[hi, cols]
            v0, v1 = v[lo, cols], v[hi, cols]
            d0, d1 = d[lo, cols], d[hi, cols]
            prefix = pb[h]
            s00 = jnp.where(lower, dot(d0, v0, 1, 1), 0.0).astype(BF16)
            s10 = dot(d1, v0, 1, 1).astype(BF16)
            s11 = jnp.where(lower, dot(d1, v1, 1, 1), 0.0).astype(BF16)
            o_dq[lo, cols] = (dot(s00, k0, 1, 0) + dot(d0, prefix, 1, 1)).astype(BF16)
            o_dq[hi, cols] = (dot(s10, k0, 1, 0) + dot(s11, k1, 1, 0) + dot(d1, prefix, 1, 1)).astype(BF16)
            dk[lo, cols] = dot(s00, q0, 0, 0) + dot(s10, q1, 0, 0)
            dk[hi, cols] = dot(s11, q1, 0, 0)
            dv[lo, cols] = dot(probs[h, 0], d0, 0, 0) + dot(probs[h, 1], d1, 0, 0)
            dv[hi, cols] = dot(probs[h, 2], d1, 0, 0)

        for src, dst, sem in ((o_gated, gated_out, 0), (o_dq, dq_out, 1), (o_gg, gg_out, 4)):
            put(src, dst, sem, half).start()
        add_up(half, True, r_b, p_b, s_b, b_s1, b_r1, b_s2, b_r2)

    @pl.loop(1, NX)
    def _(i):
        to = lax.rem(x + i, NX) * NZ + z
        remote(gs, gx_r.at[x], x_s.at[0], x_r.at[0], (to, tp)).start()

    gx_r[x] = gs[...]
    xs = gx_r.at[pl.ds(0, NX - 1)]
    xs_copy = remote(xs, xs, x_s.at[0], x_r.at[0], (lax.rem(x + 1, NX) * NZ + z, tp))
    xs_copy.wait_recv()
    gz[...] = jnp.sum(gx_r[...], axis=0)

    @pl.loop(1, NZ)
    def _(i):
        to = x * NZ + lax.rem(z + i, NZ)
        remote(gz, gz_r.at[z], z_s.at[0], z_r.at[0], (to, tp)).start()

    gz_r[z] = gz[...]

    for half in range(HALVES):
        arrived(half, s_b, b_s2, b_r2)

        @pl.loop(0, HH)
        def _(i):
            cols = cols_of(half * HH + i)
            suffix = state_of(s_b, half, i).astype(BF16)
            o_dk[:, cols] = (dk[:, cols] + dot(v[:, cols], suffix, 1, 1)).astype(BF16)
            o_dv[:, cols] = (dv[:, cols] + dot(k[:, cols], suffix, 1, 0)).astype(BF16)

        put(o_dk, dk_out, 2, half).start()
        put(o_dv, dv_out, 3, half).start()

    zs = gz_r.at[pl.ds(0, NZ - 1)]
    zs_copy = remote(zs, zs, z_s.at[0], z_r.at[0], (x * NZ + lax.rem(z + 1, NZ), tp))
    zs_copy.wait_recv()
    gain_out[...] = jnp.sum(gz_r[...], axis=0)

    for half in range(HALVES):
        others(r_a.at[half], a_s1.at[half], a_r1.at[half]).wait_send()
        others(s_a.at[half], a_s2.at[half], a_r2.at[half]).wait_send()
        others(r_b.at[half], b_s1.at[half], b_r1.at[half]).wait_send()
        others(s_b.at[half], b_s2.at[half], b_r2.at[half]).wait_send()
    peers_copy.wait_send()
    xs_copy.wait_send()
    zs_copy.wait_send()
    for half in range(HALVES):
        for src, dst, sem in (
            (o_gated, gated_out, 0), (o_dq, dq_out, 1), (o_dk, dk_out, 2), (o_dv, dv_out, 3), (o_gg, gg_out, 4),
        ):
            put(src, dst, sem, half).wait()


def body(query, key_in, value, gate, gain, grad_out):
    any_space = pl.BlockSpec(memory_space=pl.ANY)
    vmem = pl.BlockSpec(memory_space=pltpu.VMEM)
    big = jax.ShapeDtypeStruct((TOK, FEAT_DEV), BF16)
    narrow = pltpu.VMEM((TOK, FEAT_DEV), BF16)
    wide = pltpu.VMEM((TOK, FEAT_DEV), F32)
    states = pltpu.VMEM((HD * WIDTH, WIDTH), F32)
    pieces = pltpu.VMEM((HALVES, CTX, PIECE, WIDTH), F32)
    column = pltpu.VMEM((TOK, WIDTH), F32)
    tile = pltpu.VMEM((8, WIDTH), F32)
    two = pltpu.SemaphoreType.DMA((HALVES,))
    one = pltpu.SemaphoreType.DMA((1,))
    scratch = (
        [narrow] * 5
        + [wide] * 5
        + [pltpu.VMEM((HD, 3, HALF_TOK, HALF_TOK), BF16), narrow, pltpu.VMEM((HD, WIDTH, WIDTH), BF16)]
        + [narrow] * 5
        + [states, pieces, pieces, pieces] * 2
        + [column] * 4
        + [tile, pltpu.VMEM((TP, 8, WIDTH), F32)]
        + [tile, pltpu.VMEM((NX, 8, WIDTH), F32), tile, pltpu.VMEM((NZ, 8, WIDTH), F32)]
        + [pltpu.SemaphoreType.DMA((5, HALVES))] * 2
        + [two] * 8
        + [one] * 6
    )
    outs = pl.pallas_call(
        kernel,
        out_shape=[big] * 5 + [jax.ShapeDtypeStruct((8, WIDTH), F32)],
        in_specs=[any_space] * 5 + [vmem],
        out_specs=[any_space] * 5 + [vmem],
        scratch_shapes=scratch,
        compiler_params=pltpu.CompilerParams(
            collective_id=0, has_side_effects=True, vmem_limit_bytes=56 * 2**20
        ),
        name="lightning",
    )(query, key_in, value, gate, grad_out, gain.reshape(8, WIDTH))
    gated, dq, dk, dv, gg, gain_gradient = outs
    return gated, dq, dk, dv, gg, gain_gradient.reshape(-1)


def solution(mesh):
    block = P("ctx", "tp")
    specs = (block, block, block, block, P("tp"), block)
    out_specs = (block, block, block, block, block, P("tp"))
    return jax.shard_map(body, mesh=mesh, in_specs=specs, out_specs=out_specs, check_vma=False)
```

```python
import functools

import jax
import jax.numpy as jnp
from jax import lax
from jax.experimental import pallas as pl
from jax.experimental.pallas import tpu as pltpu
from jax.sharding import PartitionSpec as P

HEADS = 64
WIDTH = 128
MESH = pl.DeviceIdType.MESH
F32 = jnp.float32
BF16 = jnp.bfloat16
NX, NZ = 4, 8
CTX = NX * NZ
TP = 8
TOK = 512
HD = 8
FEAT_DEV = HD * WIDTH
HALVES = 2
HH = HD // HALVES
GROUP = 16
PIECE = WIDTH // NX
HALF_TOK = TOK // 2


def dot(a, b, ca, cb):
    return lax.dot_general(a, b, (((ca,), (cb,)), ((), ())), preferred_element_type=F32)


def kernel(
    q_in, k_in, v_in, g_in, c_in, gain_in,
    o_gated, o_dq, o_dk, o_dv, o_gg, gain_out,
    q, k, v, g, c,
    sg, w, attn, dk, dv, probs, d, pb,
    l_a, r_a, p_a, s_a, e_a, er_a, l_b, r_b, p_b, s_b, e_b, er_b,
    acc_s, acc_p, rinv_c, pm_c, st, st_r, gs, gx_r, gz, gz_r,
    gain_ref, gain_sem, in_sem,
    t_s, t_r, x_s, x_r, z_s, z_r,
    *sems,
):
    sems_a, sems_b = sems[:6], sems[6:]
    me = lax.axis_index("ctx")
    tp = lax.axis_index("tp")
    x, z = me // NZ, lax.rem(me, NZ)

    half_cols = HH * WIDTH

    def load(src, dst, sem, half):
        cols = pl.ds(half * half_cols, half_cols)
        return pltpu.make_async_copy(src.at[:, cols], dst.at[:, cols], in_sem.at[sem, half])

    pairs = ((k_in, k, 0), (v_in, v, 1), (q_in, q, 2), (g_in, g, 3), (c_in, c, 4))
    for half in range(HALVES):
        for src, dst, sem in pairs[:2]:
            load(src, dst, sem, half).start()
    for half in range(HALVES):
        for src, dst, sem in pairs[2:]:
            load(src, dst, sem, half).start()

    gain_load = pltpu.make_async_copy(gain_in, gain_ref, gain_sem.at[0])
    gain_load.start()

    barrier = pltpu.get_barrier_semaphore()

    @pl.loop(1, CTX)
    def _(i):
        pl.semaphore_signal(barrier, inc=1, device_id=(lax.rem(me + i, CTX), tp), device_id_type=MESH)

    @pl.loop(1, TP)
    def _(i):
        pl.semaphore_signal(barrier, inc=1, device_id=(me, lax.rem(tp + i, TP)), device_id_type=MESH)

    def remote(src, dst, ss, rs, to):
        return pltpu.make_async_remote_copy(
            src_ref=src, dst_ref=dst, send_sem=ss, recv_sem=rs, device_id=to, device_id_type=MESH
        )

    class Sum:
        def __init__(self, reverse, l, r, p, s, e, e_r, s1, r1, s2, r2, s3, r3):
            self.rx = NX - 1 - x if reverse else x
            self.rz = NZ - 1 - z if reverse else z
            self.reverse = reverse
            self.l, self.r, self.p, self.s, self.e, self.e_r = l, r, p, s, e, e_r
            self.up, self.across, self.down = (s1, r1), (s2, r2), (s3, r3)
            rz = self.rz
            self.wrap = (rz == 0) | (rz == 7)
            low, mid = (rz == 1) | (rz == 2), (rz == 3) | (rz == 4)
            self.all_before, self.half_before = low | mid, self.wrap
            self.first = jnp.where(low, 0, jnp.where(mid, 2, jnp.where(self.wrap, 0, 4)))
            self.kind = jnp.where((rz == 2) | (rz == 5), 0, jnp.where((rz == 1) | (rz == 6), 1, jnp.where((rz == 4) | (rz == 7), 2, 3)))
            self.partner = jnp.where((rz == 1) | (rz == 6), 7 - rz, jnp.where((rz == 2) | (rz == 5), 7 - rz, jnp.where((rz == 0) | (rz == 3), 3 - rz, 11 - rz)))

        def device(self, rx, rz):
            ctx = rx * NZ + rz
            return (CTX - 1 - ctx if self.reverse else ctx, tp)

        def home(self, kind):
            rz = self.rz
            mid = (rz >= 2) & (rz <= 5)
            outer = jnp.where(rz < 4, 2 - kind, 5 + kind)
            inner = jnp.where(mid, 6 - kind, 21 - 7 * kind)
            place_outer = lax.rem(rz, 4)
            place_inner = jnp.where(mid, rz - 2, jnp.where(rz < 2, rz, rz - 4))
            return jnp.where(kind < 2, outer, inner), jnp.where(kind < 2, place_outer, place_inner)

        def some(self, buf, sems, half):
            part = buf.at[half, pl.ds(0, GROUP - 1)]
            return remote(part, part, sems[0].at[half], sems[1].at[half], (lax.rem(me + 1, CTX), tp))

        def send(self, half):
            base = half * HH * WIDTH

            @pl.loop(0, GROUP)
            def _(i):
                kind, hx = lax.rem(i // NX + self.rz, 4), lax.rem(lax.rem(i, NX) + self.rx, NX)
                hz, place = self.home(kind)
                rows = pl.ds(pl.multiple_of(base + kind * WIDTH + hx * PIECE, PIECE), PIECE)
                slot = self.rx * 4 + place
                mine = (hx == self.rx) & (hz == self.rz)

                @pl.when(mine)
                def _():
                    self.r[half, slot] = self.l[rows, :]

                @pl.when(jnp.logical_not(mine))
                def _():
                    remote(
                        self.l.at[rows], self.r.at[half, slot], self.up[0].at[half], self.up[1].at[half],
                        self.device(hx, hz),
                    ).start()

        def across_copy(self, half):
            return remote(
                self.e.at[half], self.e_r.at[half], self.across[0].at[half], self.across[1].at[half],
                self.device(self.rx, self.partner),
            )

        def add_up(self, half):
            self.some(self.r, self.up, half).wait_recv()
            total = jnp.zeros((PIECE, WIDTH), F32)
            for row in range(NX):
                before = total
                for m in range(4):
                    if m == 2:
                        middle = total
                    self.p[half, row * 4 + m] = total
                    total = total + self.r[half, row * 4 + m]
                self.e[half, row] = jnp.where(self.all_before, total, jnp.where(self.half_before, middle, before))
            self.across_copy(half).start()

        def finish(self, half):
            self.across_copy(half).wait_recv()
            for row in range(NX):
                whole = self.e_r[half, row]
                earlier = self.e_r[half, row - 1] if row else jnp.zeros((PIECE, WIDTH), F32)
                earlier = jnp.where(self.wrap, earlier, whole)
                for m in range(4):
                    self.p[half, row * 4 + m] += earlier if m < 2 else whole
            slot = self.kind * NX + self.rx

            @pl.loop(0, GROUP)
            def _(i):
                row, m = lax.rem(i // 4 + self.rx, NX), lax.rem(i + self.rz, 4)
                to_z = self.first + m + jnp.where(self.wrap & (m >= 2), 4, 0)
                mine = (row == self.rx) & (to_z == self.rz)

                @pl.when(mine)
                def _():
                    self.s[half, slot] = self.p[half, row * 4 + m]

                @pl.when(jnp.logical_not(mine))
                def _():
                    remote(
                        self.p.at[half, row * 4 + m], self.s.at[half, slot], self.down[0].at[half],
                        self.down[1].at[half], self.device(row, to_z),
                    ).start()

        def arrived(self, half):
            self.some(self.s, self.down, half).wait_recv()

        def state(self, half, i):
            return self.s[half, pl.ds(pl.multiple_of(i * NX, NX), NX)].reshape(WIDTH, WIDTH)

        def sent(self):
            for half in range(HALVES):
                self.some(self.r, self.up, half).wait_send()
                self.across_copy(half).wait_send()
                self.some(self.s, self.down, half).wait_send()

    prefixes = Sum(False, l_a, r_a, p_a, s_a, e_a, er_a, *sems_a)
    suffixes = Sum(True, l_b, r_b, p_b, s_b, e_b, er_b, *sems_b)

    def cols_of(h):
        return pl.ds(pl.multiple_of(h * WIDTH, WIDTH), WIDTH)

    for half in range(HALVES):
        for src, dst, sem in pairs[:2]:
            load(src, dst, sem, half).wait()

        @pl.loop(half * HH, (half + 1) * HH)
        def _(h):
            cols = cols_of(h)
            l_a[cols, :] = dot(k[:, cols], v[:, cols], 0, 0)

        if half == 0:
            pl.semaphore_wait(barrier, CTX - 1 + TP - 1)
        prefixes.send(half)

    lower = lax.broadcasted_iota(jnp.int32, (HALF_TOK, HALF_TOK), 0) >= lax.broadcasted_iota(
        jnp.int32, (HALF_TOK, HALF_TOK), 1
    )
    lo, hi = pl.ds(0, HALF_TOK), pl.ds(HALF_TOK, HALF_TOK)

    gain_load.wait()
    acc_s[...] = jnp.zeros_like(acc_s)
    acc_p[...] = jnp.zeros_like(acc_p)

    def within_forward(first, last):
        @pl.loop(first, last)
        def _(h):
            cols = cols_of(h)
            q0, q1 = q[lo, cols], q[hi, cols]
            k0, k1 = k[lo, cols], k[hi, cols]
            v0, v1 = v[lo, cols], v[hi, cols]
            p00 = jnp.where(lower, dot(q0, k0, 1, 1), 0.0).astype(BF16)
            p10 = dot(q1, k0, 1, 1).astype(BF16)
            p11 = jnp.where(lower, dot(q1, k1, 1, 1), 0.0).astype(BF16)
            probs[h, 0] = p00
            probs[h, 1] = p10
            probs[h, 2] = p11
            attn[lo, cols] = dot(p00, v0, 1, 0)
            attn[hi, cols] = dot(p10, v0, 1, 0) + dot(p11, v1, 1, 0)
            gain = gain_ref[pl.ds(h, 1), :]
            for t in range(4):
                rows = pl.ds(t * 128, 128)
                gate = jax.nn.sigmoid(g[rows, cols].astype(F32))
                sg[rows, cols] = gate
                w[rows, cols] = c[rows, cols].astype(F32) * gate * gain

    for half in range(HALVES):
        for src, dst, sem in pairs[2:]:
            load(src, dst, sem, half).wait()
    within_forward(0, 4)
    prefixes.add_up(0)
    prefixes.add_up(1)
    prefixes.finish(0)
    within_forward(4, 6)
    prefixes.finish(1)
    within_forward(6, 8)

    for half in range(HALVES):
        prefixes.arrived(half)

        @pl.loop(0, HH)
        def _(i):
            h = half * HH + i
            cols = cols_of(h)
            prefix = prefixes.state(half, i).astype(BF16)
            pb[h] = prefix
            for t in range(4):
                rows = pl.ds(t * 128, 128)
                a = attn[rows, cols] + dot(q[rows, cols], prefix, 1, 0)
                attn[rows, cols] = a
                acc_s[rows, :] += a * a
                acc_p[rows, :] += a * w[rows, cols]

    for t in range(4):
        rows = pl.ds(t * 128, 128)
        st[pl.ds(t, 1), :] = jnp.sum(acc_s[rows, :].T, axis=0, keepdims=True)
        st[pl.ds(4 + t, 1), :] = jnp.sum(acc_p[rows, :].T, axis=0, keepdims=True)

    @pl.loop(1, TP)
    def _(i):
        remote(st, st_r.at[tp], t_s.at[0], t_r.at[0], (me, lax.rem(tp + i, TP))).start()

    st_r[tp] = st[...]
    peers = st_r.at[pl.ds(0, TP - 1)]
    peers_copy = remote(peers, peers, t_s.at[0], t_r.at[0], (me, lax.rem(tp + 1, TP)))
    peers_copy.wait_recv()
    sums = jnp.sum(st_r[...], axis=0)
    feat = float(HEADS * WIDTH)
    rinv = lax.rsqrt(sums[0:4] / feat + 1e-06)
    mean = sums[4:8] * rinv / feat
    for t in range(4):
        rows = pl.ds(t * 128, 128)
        rinv_c[rows, :] = jnp.broadcast_to(rinv[t : t + 1], (128, 128)).T
        pm_c[rows, :] = jnp.broadcast_to(mean[t : t + 1], (128, 128)).T

    for half in range(HALVES):
        @pl.loop(half * HH, (half + 1) * HH)
        def _(h):
            cols = cols_of(h)
            for t in range(4):
                rows = pl.ds(t * 128, 128)
                ri = rinv_c[rows, :]
                xhat = attn[rows, cols] * ri
                d[rows, cols] = (ri * (w[rows, cols] - xhat * pm_c[rows, :])).astype(BF16)
            l_b[cols, :] = dot(q[:, cols], d[:, cols], 0, 0)

        suffixes.send(half)

    @pl.loop(0, HD)
    def _(h):
        cols = cols_of(h)
        gain = gain_ref[pl.ds(h, 1), :]
        part = jnp.zeros((8, WIDTH), F32)
        for t in range(4):
            rows = pl.ds(t * 128, 128)
            xhat = attn[rows, cols] * rinv_c[rows, :]
            normed = xhat * gain
            gate = sg[rows, cols]
            cot = c[rows, cols].astype(F32)
            o_gated[rows, cols] = (normed * gate).astype(BF16)
            o_gg[rows, cols] = (cot * normed * gate * (1.0 - gate)).astype(BF16)
            part = part + jnp.sum((cot * gate * xhat).reshape(16, 8, WIDTH), axis=0)
        gs[pl.ds(h, 1), :] = jnp.sum(part, axis=0, keepdims=True)

    @pl.loop(1, NX)
    def _(i):
        to = lax.rem(x + i, NX) * NZ + z
        remote(gs, gx_r.at[x], x_s.at[0], x_r.at[0], (to, tp)).start()

    gx_r[x] = gs[...]
    xs = gx_r.at[pl.ds(0, NX - 1)]
    xs_copy = remote(xs, xs, x_s.at[0], x_r.at[0], (lax.rem(x + 1, NX) * NZ + z, tp))

    def within_backward(first, last):
        @pl.loop(first, last)
        def _(h):
            cols = cols_of(h)
            q0, q1 = q[lo, cols], q[hi, cols]
            k0, k1 = k[lo, cols], k[hi, cols]
            v0, v1 = v[lo, cols], v[hi, cols]
            d0, d1 = d[lo, cols], d[hi, cols]
            prefix = pb[h]
            s00 = jnp.where(lower, dot(d0, v0, 1, 1), 0.0).astype(BF16)
            s10 = dot(d1, v0, 1, 1).astype(BF16)
            s11 = jnp.where(lower, dot(d1, v1, 1, 1), 0.0).astype(BF16)
            o_dq[lo, cols] = (dot(s00, k0, 1, 0) + dot(d0, prefix, 1, 1)).astype(BF16)
            o_dq[hi, cols] = (dot(s10, k0, 1, 0) + dot(s11, k1, 1, 0) + dot(d1, prefix, 1, 1)).astype(BF16)
            dk[lo, cols] = dot(s00, q0, 0, 0) + dot(s10, q1, 0, 0)
            dk[hi, cols] = dot(s11, q1, 0, 0)
            dv[lo, cols] = dot(probs[h, 0], d0, 0, 0) + dot(probs[h, 1], d1, 0, 0)
            dv[hi, cols] = dot(probs[h, 2], d1, 0, 0)

    within_backward(0, 2)
    suffixes.add_up(0)
    within_backward(2, 3)
    suffixes.add_up(1)
    xs_copy.wait_recv()
    gz[...] = jnp.sum(gx_r[...], axis=0)

    @pl.loop(1, NZ)
    def _(i):
        to = x * NZ + lax.rem(z + i, NZ)
        remote(gz, gz_r.at[z], z_s.at[0], z_r.at[0], (to, tp)).start()

    gz_r[z] = gz[...]
    suffixes.finish(0)
    within_backward(3, 5)
    suffixes.finish(1)
    within_backward(5, 8)

    for half in range(HALVES):
        suffixes.arrived(half)

        @pl.loop(0, HH)
        def _(i):
            cols = cols_of(half * HH + i)
            suffix = suffixes.state(half, i).astype(BF16)
            o_dk[:, cols] = (dk[:, cols] + dot(v[:, cols], suffix, 1, 1)).astype(BF16)
            o_dv[:, cols] = (dv[:, cols] + dot(k[:, cols], suffix, 1, 0)).astype(BF16)

    zs = gz_r.at[pl.ds(0, NZ - 1)]
    zs_copy = remote(zs, zs, z_s.at[0], z_r.at[0], (x * NZ + lax.rem(z + 1, NZ), tp))
    zs_copy.wait_recv()
    gain_out[...] = jnp.sum(gz_r[...], axis=0)

    prefixes.sent()
    suffixes.sent()
    peers_copy.wait_send()
    xs_copy.wait_send()
    zs_copy.wait_send()


def store(*refs):
    n = len(refs) // 2
    sem = refs[-1]
    srcs, dsts = refs[:n], refs[n:2 * n]

    def parts(start):
        for i, (src, dst) in enumerate(zip(srcs, dsts)):
            if src.shape[0] == TOK:
                for half in range(HALVES):
                    rows = pl.ds(half * HALF_TOK, HALF_TOK)
                    start(pltpu.make_async_copy(src.at[rows], dst.at[rows], sem.at[i, half]))
            else:
                start(pltpu.make_async_copy(src, dst, sem.at[i, 0]))

    parts(lambda copy: copy.start())
    parts(lambda copy: copy.wait())


def body(query, key_in, value, gate, gain, grad_out):
    any_space = pl.BlockSpec(memory_space=pl.ANY)
    vmem = pl.BlockSpec(memory_space=pltpu.VMEM)
    big = jax.ShapeDtypeStruct((TOK, FEAT_DEV), BF16)
    narrow = pltpu.VMEM((TOK, FEAT_DEV), BF16)
    wide = pltpu.VMEM((TOK, FEAT_DEV), F32)
    states = pltpu.VMEM((HD * WIDTH, WIDTH), F32)
    pieces = pltpu.VMEM((HALVES, GROUP, PIECE, WIDTH), F32)
    sums = pltpu.VMEM((HALVES, NX, PIECE, WIDTH), F32)
    column = pltpu.VMEM((TOK, WIDTH), F32)
    tile = pltpu.VMEM((8, WIDTH), F32)
    two = pltpu.SemaphoreType.DMA((HALVES,))
    one = pltpu.SemaphoreType.DMA((1,))
    scratch = (
        [narrow] * 5
        + [wide] * 5
        + [pltpu.VMEM((HD, 3, HALF_TOK, HALF_TOK), BF16), narrow, pltpu.VMEM((HD, WIDTH, WIDTH), BF16)]
        + [states, pieces, pieces, pieces, sums, sums] * 2
        + [column] * 4
        + [tile, pltpu.VMEM((TP, 8, WIDTH), F32)]
        + [tile, pltpu.VMEM((NX, 8, WIDTH), F32), tile, pltpu.VMEM((NZ, 8, WIDTH), F32)]
        + [tile, one, pltpu.SemaphoreType.DMA((5, HALVES))]
        + [one] * 6
        + [two] * 12
    )
    outs = pl.pallas_call(
        kernel,
        out_shape=[narrow] * 5 + [tile],
        in_specs=[any_space] * 6,
        out_specs=[vmem] * 6,
        scratch_shapes=scratch,
        compiler_params=pltpu.CompilerParams(
            collective_id=0, has_side_effects=True, vmem_limit_bytes=56 * 2**20
        ),
        name="lightning",
    )(query, key_in, value, gate, grad_out, gain.reshape(8, WIDTH))
    gated, dq, dk, dv, gg, gain_gradient = pl.pallas_call(
        store,
        out_shape=[big] * 5 + [jax.ShapeDtypeStruct((8, WIDTH), F32)],
        in_specs=[any_space] * 6,
        out_specs=[any_space] * 6,
        scratch_shapes=[pltpu.SemaphoreType.DMA((6, HALVES))],
        compiler_params=pltpu.CompilerParams(vmem_limit_bytes=4 * 2**20),
        name="store",
    )(*outs)
    return gated, dq, dk, dv, gg, gain_gradient.reshape(-1)


def solution(mesh):
    block = P("ctx", "tp")
    specs = (block, block, block, block, P("tp"), block)
    out_specs = (block, block, block, block, block, P("tp"))
    return jax.shard_map(body, mesh=mesh, in_specs=specs, out_specs=out_specs, check_vma=False)
```

```python
import functools

import jax
import jax.numpy as jnp
from jax import lax
from jax.experimental import pallas as pl
from jax.experimental.pallas import tpu as pltpu
from jax.sharding import PartitionSpec as P

HEADS = 64
WIDTH = 128
MESH = pl.DeviceIdType.MESH
F32 = jnp.float32
BF16 = jnp.bfloat16
NX, NZ = 4, 8
CTX = NX * NZ
TP = 8
TOK = 512
HD = 8
FEAT_DEV = HD * WIDTH
HALVES = 2
PARTS = 4
HH = HD // PARTS
FAR_FIRST = (2, 1, 3, 0)
GROUP = 16
PIECE = HH * WIDTH // GROUP
HALF_TOK = TOK // 2


def dot(a, b, ca, cb):
    return lax.dot_general(a, b, (((ca,), (cb,)), ((), ())), preferred_element_type=F32)


def kernel(
    q_in, k_in, v_in, g_in, c_in, gain_in,
    o_gated, o_dq, o_dk, o_dv, o_gg, gain_out,
    q, k, v, g, c,
    sg, w, attn, dk, dv, probs, d, pb,
    l_a, r_a, p_a, s_a, e_a, er_a, l_b, r_b, p_b, s_b, e_b, er_b,
    acc_s, acc_p, rinv_c, pm_c, st, st_r, gs, gx_r, gz, gz_r,
    gain_ref, gain_sem, in_sem,
    t_s, t_r, x_s, x_r, z_s, z_r,
    *sems,
):
    sems_a, sems_b = sems[:6], sems[6:]
    me = lax.axis_index("ctx")
    tp = lax.axis_index("tp")
    x, z = me // NZ, lax.rem(me, NZ)

    def load(src, dst, sem, part):
        cols = pl.ds(part * HH * WIDTH, HH * WIDTH)
        return pltpu.make_async_copy(src.at[:, cols], dst.at[:, cols], in_sem.at[sem, part])

    pairs = ((k_in, k, 0), (v_in, v, 1), (q_in, q, 2), (g_in, g, 3), (c_in, c, 4))
    for part in range(PARTS):
        for src, dst, sem in pairs[:2]:
            load(src, dst, sem, part).start()

    barrier = pltpu.get_barrier_semaphore()
    for i in range(1, CTX):
        pl.semaphore_signal(barrier, inc=1, device_id=(lax.rem(me + i, CTX), tp), device_id_type=MESH)
    for i in range(1, TP):
        pl.semaphore_signal(barrier, inc=1, device_id=(me, lax.rem(tp + i, TP)), device_id_type=MESH)

    for part in range(PARTS):
        for src, dst, sem in pairs[2:]:
            load(src, dst, sem, part).start()
    gain_load = pltpu.make_async_copy(gain_in, gain_ref, gain_sem.at[0])
    gain_load.start()

    def remote(src, dst, ss, rs, to):
        return pltpu.make_async_remote_copy(
            src_ref=src, dst_ref=dst, send_sem=ss, recv_sem=rs, device_id=to, device_id_type=MESH
        )

    class Sum:
        def __init__(self, reverse, l, r, p, s, e, e_r, s1, r1, s2, r2, s3, r3):
            self.rx = NX - 1 - x if reverse else x
            self.rz = NZ - 1 - z if reverse else z
            self.reverse = reverse
            self.l, self.r, self.p, self.s, self.e, self.e_r = l, r, p, s, e, e_r
            self.up, self.across, self.down = (s1, r1), (s2, r2), (s3, r3)

        def device(self, rx, rz):
            ctx = rx * NZ + rz
            return (CTX - 1 - ctx if self.reverse else ctx, tp)

        def some(self, buf, sems, part):
            most = buf.at[part, pl.ds(0, GROUP - 1)]
            return remote(most, most, sems[0].at[part], sems[1].at[part], (lax.rem(me + 1, CTX), tp))

        def home(self, part, kind):
            turn = part % 2 + 2 * (kind // 2)
            second = lax.rem(self.rz - turn + NZ, NZ) // 4
            start = lax.rem(turn + 4 * second, NZ)
            off = jnp.where(second == 0, 2, 1) if kind % 2 == 0 else jnp.where(second == 0, 1, 2)
            ahead = jnp.maximum(start - 4, 0)
            place = jnp.where(self.rz < ahead, self.rz, self.rz - start + ahead)
            return lax.rem(start + off, NZ), place

        def role(self, part):
            turn = part % 2
            u = lax.rem(self.rz - turn + NZ, NZ)
            outer_a, outer_b, inner_a = (u == 2) | (u == 5), (u == 1) | (u == 6), (u == 4) | (u == 7)
            kind = jnp.where(outer_a, 0, jnp.where(outer_b, 1, jnp.where(inner_a, 2, 3)))
            partner = jnp.where(kind < 2, 7 - u, jnp.where(kind == 2, 11 - u, 3 - u))
            base = jnp.where((u == 1) | (u == 2), 0, jnp.where((u == 5) | (u == 6), 4, jnp.where((u == 3) | (u == 4), 2, 6)))
            start = lax.rem(base + turn, NZ)
            return kind, lax.rem(partner + turn, NZ), start, jnp.maximum(start - 4, 0)

        def send(self, part):
            first = part * HH * WIDTH
            homes = [self.home(part, kind) for kind in range(4)]
            for i in FAR_FIRST:
                hx = lax.rem(self.rx + i, NX)
                for kind, (hz, place) in enumerate(homes):
                    rows = pl.ds(pl.multiple_of(first + (kind * NX + hx) * PIECE, PIECE), PIECE)
                    slot = self.rx * 4 + place

                    def go():
                        remote(
                            self.l.at[rows], self.r.at[part, slot], self.up[0].at[part], self.up[1].at[part],
                            self.device(hx, hz),
                        ).start()

                    if i:
                        go()
                    else:
                        pl.when(hz != self.rz)(go)

                        @pl.when(hz == self.rz)
                        def _():
                            self.r[part, slot] = self.l[rows, :]

        def across_copy(self, part, partner):
            return remote(
                self.e.at[part], self.e_r.at[part], self.across[0].at[part], self.across[1].at[part],
                self.device(self.rx, partner),
            )

        def add_up(self, part):
            _, partner, start, ahead = self.role(part)
            self.some(self.r, self.up, part).wait_recv()
            total = jnp.zeros((PIECE, WIDTH), F32)
            for slot in range(GROUP):
                self.p[part, slot] = total
                total = total + self.r[part, slot]
            self.p[part, GROUP] = total
            cut = jnp.where(start < 4, 4, ahead)
            for row in range(NX):
                self.e[part, row] = self.p[part, row * 4 + cut]
            self.across_copy(part, partner).start()

        def finish(self, part):
            kind, partner, start, ahead = self.role(part)
            self.across_copy(part, partner).wait_recv()
            for row in range(NX):
                whole = self.e_r[part, row]
                earlier = self.e_r[part, row - 1] if row else jnp.zeros((PIECE, WIDTH), F32)
                for m in range(4):
                    self.p[part, row * 4 + m] += jnp.where(m < ahead, earlier, whole)
            slot = kind * NX + self.rx
            for i in FAR_FIRST:
                row = lax.rem(self.rx + i, NX)
                for m in range(4):
                    to_z = jnp.where(m < ahead, m, start + m - ahead)
                    done = self.p.at[part, row * 4 + m]

                    def go():
                        remote(
                            done, self.s.at[part, slot], self.down[0].at[part], self.down[1].at[part],
                            self.device(row, to_z),
                        ).start()

                    if i:
                        go()
                    else:
                        pl.when(to_z != self.rz)(go)

                        @pl.when(to_z == self.rz)
                        def _():
                            self.s[part, slot] = self.p[part, row * 4 + m]

        def arrived(self, part):
            self.some(self.s, self.down, part).wait_recv()

        def state(self, part, i):
            whole = WIDTH // PIECE
            return self.s[part, pl.ds(pl.multiple_of(i * whole, whole), whole)].reshape(WIDTH, WIDTH)

        def sent(self):
            for part in range(PARTS):
                self.some(self.r, self.up, part).wait_send()
                self.across_copy(part, 0).wait_send()
                self.some(self.s, self.down, part).wait_send()

    prefixes = Sum(False, l_a, r_a, p_a, s_a, e_a, er_a, *sems_a)
    suffixes = Sum(True, l_b, r_b, p_b, s_b, e_b, er_b, *sems_b)

    def cols_of(h):
        return pl.ds(pl.multiple_of(h * WIDTH, WIDTH), WIDTH)

    for part in range(PARTS):
        for src, dst, sem in pairs[:2]:
            load(src, dst, sem, part).wait()

        @pl.loop(part * HH, (part + 1) * HH)
        def _(h):
            cols = cols_of(h)
            l_a[cols, :] = dot(k[:, cols], v[:, cols], 0, 0)

        if part == 0:
            pl.semaphore_wait(barrier, CTX - 1 + TP - 1)
        prefixes.send(part)

    lower = lax.broadcasted_iota(jnp.int32, (HALF_TOK, HALF_TOK), 0) >= lax.broadcasted_iota(
        jnp.int32, (HALF_TOK, HALF_TOK), 1
    )
    lo, hi = pl.ds(0, HALF_TOK), pl.ds(HALF_TOK, HALF_TOK)

    gain_load.wait()
    acc_s[...] = jnp.zeros_like(acc_s)
    acc_p[...] = jnp.zeros_like(acc_p)

    def within_forward(first, last):
        @pl.loop(first, last)
        def _(h):
            cols = cols_of(h)
            q0, q1 = q[lo, cols], q[hi, cols]
            k0, k1 = k[lo, cols], k[hi, cols]
            v0, v1 = v[lo, cols], v[hi, cols]
            p00 = jnp.where(lower, dot(q0, k0, 1, 1), 0.0).astype(BF16)
            p10 = dot(q1, k0, 1, 1).astype(BF16)
            p11 = jnp.where(lower, dot(q1, k1, 1, 1), 0.0).astype(BF16)
            probs[h, 0] = p00
            probs[h, 1] = p10
            probs[h, 2] = p11
            attn[lo, cols] = dot(p00, v0, 1, 0)
            attn[hi, cols] = dot(p10, v0, 1, 0) + dot(p11, v1, 1, 0)
            gain = gain_ref[pl.ds(h, 1), :]
            for t in range(4):
                rows = pl.ds(t * 128, 128)
                gate = jax.nn.sigmoid(g[rows, cols].astype(F32))
                sg[rows, cols] = gate
                w[rows, cols] = c[rows, cols].astype(F32) * gate * gain

    for part in range(PARTS):
        for src, dst, sem in pairs[2:]:
            load(src, dst, sem, part).wait()
    within_forward(0, 4)
    for part in range(PARTS):
        prefixes.add_up(part)
    for part in range(PARTS):
        prefixes.finish(part)
        within_forward(4 + part, 5 + part)

    for part in range(PARTS):
        prefixes.arrived(part)

        @pl.loop(0, HH)
        def _(i):
            h = part * HH + i
            cols = cols_of(h)
            prefix = prefixes.state(part, i).astype(BF16)
            pb[h] = prefix
            for t in range(4):
                rows = pl.ds(t * 128, 128)
                a = attn[rows, cols] + dot(q[rows, cols], prefix, 1, 0)
                attn[rows, cols] = a
                acc_s[rows, :] += a * a
                acc_p[rows, :] += a * w[rows, cols]

    for t in range(4):
        rows = pl.ds(t * 128, 128)
        st[pl.ds(t, 1), :] = jnp.sum(acc_s[rows, :].T, axis=0, keepdims=True)
        st[pl.ds(4 + t, 1), :] = jnp.sum(acc_p[rows, :].T, axis=0, keepdims=True)

    @pl.loop(1, TP)
    def _(i):
        remote(st, st_r.at[tp], t_s.at[0], t_r.at[0], (me, lax.rem(tp + i, TP))).start()

    st_r[tp] = st[...]
    peers = st_r.at[pl.ds(0, TP - 1)]
    peers_copy = remote(peers, peers, t_s.at[0], t_r.at[0], (me, lax.rem(tp + 1, TP)))
    peers_copy.wait_recv()
    sums = jnp.sum(st_r[...], axis=0)
    feat = float(HEADS * WIDTH)
    rinv = lax.rsqrt(sums[0:4] / feat + 1e-06)
    mean = sums[4:8] * rinv / feat
    for t in range(4):
        rows = pl.ds(t * 128, 128)
        rinv_c[rows, :] = jnp.broadcast_to(rinv[t : t + 1], (128, 128)).T
        pm_c[rows, :] = jnp.broadcast_to(mean[t : t + 1], (128, 128)).T

    for part in range(PARTS):
        @pl.loop(part * HH, (part + 1) * HH)
        def _(h):
            cols = cols_of(h)
            for t in range(4):
                rows = pl.ds(t * 128, 128)
                ri = rinv_c[rows, :]
                xhat = attn[rows, cols] * ri
                d[rows, cols] = (ri * (w[rows, cols] - xhat * pm_c[rows, :])).astype(BF16)
            l_b[cols, :] = dot(q[:, cols], d[:, cols], 0, 0)

        suffixes.send(part)

    @pl.loop(0, HD)
    def _(h):
        cols = cols_of(h)
        gain = gain_ref[pl.ds(h, 1), :]
        part = jnp.zeros((8, WIDTH), F32)
        for t in range(4):
            rows = pl.ds(t * 128, 128)
            xhat = attn[rows, cols] * rinv_c[rows, :]
            normed = xhat * gain
            gate = sg[rows, cols]
            cot = c[rows, cols].astype(F32)
            o_gated[rows, cols] = (normed * gate).astype(BF16)
            o_gg[rows, cols] = (cot * normed * gate * (1.0 - gate)).astype(BF16)
            part = part + jnp.sum((cot * gate * xhat).reshape(16, 8, WIDTH), axis=0)
        gs[pl.ds(h, 1), :] = jnp.sum(part, axis=0, keepdims=True)

    @pl.loop(1, NX)
    def _(i):
        to = lax.rem(x + i, NX) * NZ + z
        remote(gs, gx_r.at[x], x_s.at[0], x_r.at[0], (to, tp)).start()

    gx_r[x] = gs[...]
    xs = gx_r.at[pl.ds(0, NX - 1)]
    xs_copy = remote(xs, xs, x_s.at[0], x_r.at[0], (lax.rem(x + 1, NX) * NZ + z, tp))

    def within_backward(first, last):
        @pl.loop(first, last)
        def _(h):
            cols = cols_of(h)
            q0, q1 = q[lo, cols], q[hi, cols]
            k0, k1 = k[lo, cols], k[hi, cols]
            v0, v1 = v[lo, cols], v[hi, cols]
            d0, d1 = d[lo, cols], d[hi, cols]
            prefix = pb[h]
            s00 = jnp.where(lower, dot(d0, v0, 1, 1), 0.0).astype(BF16)
            s10 = dot(d1, v0, 1, 1).astype(BF16)
            s11 = jnp.where(lower, dot(d1, v1, 1, 1), 0.0).astype(BF16)
            o_dq[lo, cols] = (dot(s00, k0, 1, 0) + dot(d0, prefix, 1, 1)).astype(BF16)
            o_dq[hi, cols] = (dot(s10, k0, 1, 0) + dot(s11, k1, 1, 0) + dot(d1, prefix, 1, 1)).astype(BF16)
            dk[lo, cols] = dot(s00, q0, 0, 0) + dot(s10, q1, 0, 0)
            dk[hi, cols] = dot(s11, q1, 0, 0)
            dv[lo, cols] = dot(probs[h, 0], d0, 0, 0) + dot(probs[h, 1], d1, 0, 0)
            dv[hi, cols] = dot(probs[h, 2], d1, 0, 0)

    within_backward(0, 2)
    for part in range(PARTS):
        suffixes.add_up(part)
    xs_copy.wait_recv()
    gz[...] = jnp.sum(gx_r[...], axis=0)

    @pl.loop(1, NZ)
    def _(i):
        to = x * NZ + lax.rem(z + i, NZ)
        remote(gz, gz_r.at[z], z_s.at[0], z_r.at[0], (to, tp)).start()

    gz_r[z] = gz[...]
    suffixes.finish(0)
    within_backward(2, 3)
    suffixes.finish(1)
    within_backward(3, 4)
    suffixes.finish(2)
    within_backward(4, 5)
    suffixes.finish(3)
    within_backward(5, 8)

    for part in range(PARTS):
        suffixes.arrived(part)

        @pl.loop(0, HH)
        def _(i):
            cols = cols_of(part * HH + i)
            suffix = suffixes.state(part, i).astype(BF16)
            o_dk[:, cols] = (dk[:, cols] + dot(v[:, cols], suffix, 1, 1)).astype(BF16)
            o_dv[:, cols] = (dv[:, cols] + dot(k[:, cols], suffix, 1, 0)).astype(BF16)

    zs = gz_r.at[pl.ds(0, NZ - 1)]
    zs_copy = remote(zs, zs, z_s.at[0], z_r.at[0], (x * NZ + lax.rem(z + 1, NZ), tp))
    zs_copy.wait_recv()
    gain_out[...] = jnp.sum(gz_r[...], axis=0)

    prefixes.sent()
    suffixes.sent()
    peers_copy.wait_send()
    xs_copy.wait_send()
    zs_copy.wait_send()


def store(*refs):
    n = len(refs) // 2
    sem = refs[-1]
    srcs, dsts = refs[:n], refs[n:2 * n]

    def parts(start):
        for i, (src, dst) in enumerate(zip(srcs, dsts)):
            if src.shape[0] == TOK:
                for half in range(HALVES):
                    rows = pl.ds(half * HALF_TOK, HALF_TOK)
                    start(pltpu.make_async_copy(src.at[rows], dst.at[rows], sem.at[i, half]))
            else:
                start(pltpu.make_async_copy(src, dst, sem.at[i, 0]))

    parts(lambda copy: copy.start())
    parts(lambda copy: copy.wait())


def body(query, key_in, value, gate, gain, grad_out):
    any_space = pl.BlockSpec(memory_space=pl.ANY)
    vmem = pl.BlockSpec(memory_space=pltpu.VMEM)
    big = jax.ShapeDtypeStruct((TOK, FEAT_DEV), BF16)
    narrow = pltpu.VMEM((TOK, FEAT_DEV), BF16)
    wide = pltpu.VMEM((TOK, FEAT_DEV), F32)
    states = pltpu.VMEM((HD * WIDTH, WIDTH), F32)
    pieces = pltpu.VMEM((PARTS, GROUP, PIECE, WIDTH), F32)
    totals = pltpu.VMEM((PARTS, GROUP + 1, PIECE, WIDTH), F32)
    sums = pltpu.VMEM((PARTS, NX, PIECE, WIDTH), F32)
    column = pltpu.VMEM((TOK, WIDTH), F32)
    tile = pltpu.VMEM((8, WIDTH), F32)
    each = pltpu.SemaphoreType.DMA((PARTS,))
    one = pltpu.SemaphoreType.DMA((1,))
    scratch = (
        [narrow] * 5
        + [wide] * 5
        + [pltpu.VMEM((HD, 3, HALF_TOK, HALF_TOK), BF16), narrow, pltpu.VMEM((HD, WIDTH, WIDTH), BF16)]
        + [states, pieces, totals, pieces, sums, sums] * 2
        + [column] * 4
        + [tile, pltpu.VMEM((TP, 8, WIDTH), F32)]
        + [tile, pltpu.VMEM((NX, 8, WIDTH), F32), tile, pltpu.VMEM((NZ, 8, WIDTH), F32)]
        + [tile, one, pltpu.SemaphoreType.DMA((5, PARTS))]
        + [one] * 6
        + [each] * 12
    )
    outs = pl.pallas_call(
        kernel,
        out_shape=[narrow] * 5 + [tile],
        in_specs=[any_space] * 6,
        out_specs=[vmem] * 6,
        scratch_shapes=scratch,
        compiler_params=pltpu.CompilerParams(
            collective_id=0, has_side_effects=True, vmem_limit_bytes=56 * 2**20
        ),
        name="lightning",
    )(query, key_in, value, gate, grad_out, gain.reshape(8, WIDTH))
    gated, dq, dk, dv, gg, gain_gradient = pl.pallas_call(
        store,
        out_shape=[big] * 5 + [jax.ShapeDtypeStruct((8, WIDTH), F32)],
        in_specs=[any_space] * 6,
        out_specs=[any_space] * 6,
        scratch_shapes=[pltpu.SemaphoreType.DMA((6, HALVES))],
        compiler_params=pltpu.CompilerParams(vmem_limit_bytes=4 * 2**20),
        name="store",
    )(*outs)
    return gated, dq, dk, dv, gg, gain_gradient.reshape(-1)


def solution(mesh):
    block = P("ctx", "tp")
    specs = (block, block, block, block, P("tp"), block)
    out_specs = (block, block, block, block, block, P("tp"))
    return jax.shard_map(body, mesh=mesh, in_specs=specs, out_specs=out_specs, check_vma=False)
```

```python
import functools

import jax
import jax.numpy as jnp
from jax import lax
from jax.experimental import pallas as pl
from jax.experimental.pallas import tpu as pltpu
from jax.sharding import PartitionSpec as P

HEADS = 64
WIDTH = 128
MESH = pl.DeviceIdType.MESH
F32 = jnp.float32
BF16 = jnp.bfloat16
NX, NZ = 4, 8
CTX = NX * NZ
TP = 8
TOK = 512
HD = 8
FEAT_DEV = HD * WIDTH
HALVES = 2
PARTS = 4
HH = HD // PARTS
FAR_FIRST = (2, 1, 3, 0)
REACH = [(dx, dz) for dx in FAR_FIRST for dz in (2, 6, 1, 7, 0) if dx or dz] + [(0, 4), (0, 3), (0, 5)]
PEERS = [(2, 1), (2, 0), (1, 1), (3, 1), (1, 0), (3, 0), (0, 1)]
GROUP = 16
PIECE = HH * WIDTH // GROUP
HALF_TOK = TOK // 2


def dot(a, b, ca, cb):
    return lax.dot_general(a, b, (((ca,), (cb,)), ((), ())), preferred_element_type=F32)


def kernel(
    q_in, k_in, v_in, g_in, c_in, gain_in,
    o_gated, o_dq, o_dk, o_dv, o_gg, gain_out,
    q, k, v, g, c,
    sg, w, attn, dk, dv, probs, d, pb,
    l_a, r_a, p_a, s_a, e_a, er_a, l_b, r_b, p_b, s_b, e_b, er_b,
    acc_s, acc_p, rinv_c, pm_c, st, st_r, gs, gx_r, gz, gz_r,
    gain_ref, gain_sem, in_sem,
    t_s, t_r, x_s, x_r, z_s, z_r,
    *sems,
):
    sems_a, sems_b = sems[:6], sems[6:]
    me = lax.axis_index("ctx")
    tp = lax.axis_index("tp")
    x, z = me // NZ, lax.rem(me, NZ)

    def peer(dy, dc):
        return lax.rem(tp // 2 + dy, TP // 2) * 2 + lax.rem(lax.rem(tp, 2) + dc, 2)

    def load(src, dst, sem, part):
        cols = pl.ds(part * HH * WIDTH, HH * WIDTH)
        return pltpu.make_async_copy(src.at[:, cols], dst.at[:, cols], in_sem.at[sem, part])

    pairs = ((k_in, k, 0), (v_in, v, 1), (q_in, q, 2), (g_in, g, 3), (c_in, c, 4))
    for part in range(PARTS):
        for src, dst, sem in pairs[:2]:
            load(src, dst, sem, part).start()

    barrier = pltpu.get_barrier_semaphore()
    for dx, dz in REACH:
        to = lax.rem(x + dx, NX) * NZ + lax.rem(z + dz, NZ)
        pl.semaphore_signal(barrier, inc=1, device_id=(to, tp), device_id_type=MESH)
    for dy, dc in PEERS:
        pl.semaphore_signal(barrier, inc=1, device_id=(me, peer(dy, dc)), device_id_type=MESH)

    for part in range(PARTS):
        for src, dst, sem in pairs[2:]:
            load(src, dst, sem, part).start()
    gain_load = pltpu.make_async_copy(gain_in, gain_ref, gain_sem.at[0])
    gain_load.start()

    def remote(src, dst, ss, rs, to):
        return pltpu.make_async_remote_copy(
            src_ref=src, dst_ref=dst, send_sem=ss, recv_sem=rs, device_id=to, device_id_type=MESH
        )

    class Sum:
        def __init__(self, reverse, l, r, p, s, e, e_r, s1, r1, s2, r2, s3, r3):
            self.rx = NX - 1 - x if reverse else x
            self.rz = NZ - 1 - z if reverse else z
            self.reverse = reverse
            self.l, self.r, self.p, self.s, self.e, self.e_r = l, r, p, s, e, e_r
            self.up, self.across, self.down = (s1, r1), (s2, r2), (s3, r3)

        def device(self, rx, rz):
            ctx = rx * NZ + rz
            return (CTX - 1 - ctx if self.reverse else ctx, tp)

        def some(self, buf, sems, part):
            most = buf.at[part, pl.ds(0, GROUP - 1)]
            return remote(most, most, sems[0].at[part], sems[1].at[part], (lax.rem(me + 1, CTX), tp))

        def order(self, turn):
            u = lax.rem(self.rz - turn + NZ, NZ)
            second, place = u // 4, lax.rem(u, 4)
            outer = (place == 0) | (place == 3)
            low = (place < 2) == (second == 0)
            far = jnp.where(outer, jnp.where(low, 0, 1), jnp.where((lax.rem(u - 2 + NZ, NZ) < 4) == (lax.rem(u - 2 + NZ, 4) < 2), 2, 3))
            inner_second, inner_place = lax.rem(u - 2 + NZ, NZ) // 4, lax.rem(u - 2 + NZ, 4)
            stay = jnp.where(
                outer,
                jnp.where((inner_place == 2) == (inner_second == 0), 2, 3),
                jnp.where((place == 2) == (second == 0), 0, 1),
            )
            return far, (far + 1 - 2 * lax.rem(far, 2), stay + 1 - 2 * lax.rem(stay, 2), stay)

        def home(self, part, kind):
            turn = part % 2 + 2 * (kind // 2)
            second = lax.rem(self.rz - turn + NZ, NZ) // 4
            start = lax.rem(turn + 4 * second, NZ)
            off = jnp.where(lax.rem(kind, 2) == second, 2, 1)
            ahead = jnp.maximum(start - 4, 0)
            place = jnp.where(self.rz < ahead, self.rz, self.rz - start + ahead)
            return lax.rem(start + off, NZ), place

        def role(self, part):
            turn = part % 2
            u = lax.rem(self.rz - turn + NZ, NZ)
            outer_a, outer_b, inner_a = (u == 2) | (u == 5), (u == 1) | (u == 6), (u == 4) | (u == 7)
            kind = jnp.where(outer_a, 0, jnp.where(outer_b, 1, jnp.where(inner_a, 2, 3)))
            partner = jnp.where(kind < 2, 7 - u, jnp.where(kind == 2, 11 - u, 3 - u))
            base = jnp.where((u == 1) | (u == 2), 0, jnp.where((u == 5) | (u == 6), 4, jnp.where((u == 3) | (u == 4), 2, 6)))
            start = lax.rem(base + turn, NZ)
            return kind, lax.rem(partner + turn, NZ), start, jnp.maximum(start - 4, 0)

        def send(self, part):
            first = part * HH * WIDTH
            turn = part % 2
            far, near = self.order(turn)
            homes = [(kind, *self.home(part, kind)) for kind in (far, *near)]
            for i in FAR_FIRST:
                hx = lax.rem(self.rx + i, NX)
                for kind, hz, place in homes:
                    rows = pl.ds(pl.multiple_of(first + (kind * NX + hx) * PIECE, PIECE), PIECE)
                    slot = self.rx * 4 + place

                    def go():
                        remote(
                            self.l.at[rows], self.r.at[part, slot], self.up[0].at[part], self.up[1].at[part],
                            self.device(hx, hz),
                        ).start()

                    if i:
                        go()
                    else:
                        pl.when(hz != self.rz)(go)

                        @pl.when(hz == self.rz)
                        def _():
                            self.r[part, slot] = self.l[rows, :]

        def across_copy(self, part, partner):
            return remote(
                self.e.at[part], self.e_r.at[part], self.across[0].at[part], self.across[1].at[part],
                self.device(self.rx, partner),
            )

        def add_up(self, part):
            _, partner, start, ahead = self.role(part)
            self.some(self.r, self.up, part).wait_recv()
            total = jnp.zeros((PIECE, WIDTH), F32)
            for slot in range(GROUP):
                self.p[part, slot] = total
                total = total + self.r[part, slot]
            self.p[part, GROUP] = total
            cut = jnp.where(start < 4, 4, ahead)
            for row in range(NX):
                self.e[part, row] = self.p[part, row * 4 + cut]
            self.across_copy(part, partner).start()

        def finish(self, part):
            kind, partner, start, ahead = self.role(part)
            self.across_copy(part, partner).wait_recv()
            for row in range(NX):
                whole = self.e_r[part, row]
                earlier = self.e_r[part, row - 1] if row else jnp.zeros((PIECE, WIDTH), F32)
                for m in range(4):
                    self.p[part, row * 4 + m] += jnp.where(m < ahead, earlier, whole)
            slot = kind * NX + self.rx
            off = lax.rem(self.rz - start + NZ, NZ)
            for i in FAR_FIRST:
                row = lax.rem(self.rx + i, NX)
                for step in (3, 0, 2, 1):
                    to_z = lax.rem(start + jnp.where(off == 1, step, 3 - step), NZ)
                    m = jnp.where(to_z < ahead, to_z, to_z - start + ahead)
                    done = self.p.at[part, row * 4 + m]

                    def go():
                        remote(
                            done, self.s.at[part, slot], self.down[0].at[part], self.down[1].at[part],
                            self.device(row, to_z),
                        ).start()

                    if i:
                        go()
                    else:
                        pl.when(to_z != self.rz)(go)

                        @pl.when(to_z == self.rz)
                        def _():
                            self.s[part, slot] = self.p[part, row * 4 + m]

        def arrived(self, part):
            self.some(self.s, self.down, part).wait_recv()

        def state(self, part, i):
            whole = WIDTH // PIECE
            return self.s[part, i * whole : (i + 1) * whole].reshape(WIDTH, WIDTH)

        def sent(self):
            for part in range(PARTS):
                self.some(self.r, self.up, part).wait_send()
                self.across_copy(part, 0).wait_send()
                self.some(self.s, self.down, part).wait_send()

    prefixes = Sum(False, l_a, r_a, p_a, s_a, e_a, er_a, *sems_a)
    suffixes = Sum(True, l_b, r_b, p_b, s_b, e_b, er_b, *sems_b)

    def cols_of(h):
        return pl.ds(h * WIDTH if isinstance(h, int) else pl.multiple_of(h * WIDTH, WIDTH), WIDTH)

    for part in range(PARTS):
        for src, dst, sem in pairs[:2]:
            load(src, dst, sem, part).wait()

        for h in range(part * HH, (part + 1) * HH):
            cols = cols_of(h)
            l_a[cols, :] = dot(k[:, cols], v[:, cols], 0, 0)

        if part == 0:
            pl.semaphore_wait(barrier, len(REACH) + len(PEERS))
        prefixes.send(part)

    lower = lax.broadcasted_iota(jnp.int32, (HALF_TOK, HALF_TOK), 0) >= lax.broadcasted_iota(
        jnp.int32, (HALF_TOK, HALF_TOK), 1
    )
    lo, hi = pl.ds(0, HALF_TOK), pl.ds(HALF_TOK, HALF_TOK)

    gain_load.wait()
    acc_s[...] = jnp.zeros_like(acc_s)
    acc_p[...] = jnp.zeros_like(acc_p)

    def within_forward(first, last):
        @pl.loop(first, last)
        def _(h):
            cols = cols_of(h)
            q0, q1 = q[lo, cols], q[hi, cols]
            k0, k1 = k[lo, cols], k[hi, cols]
            v0, v1 = v[lo, cols], v[hi, cols]
            p00 = jnp.where(lower, dot(q0, k0, 1, 1), 0.0).astype(BF16)
            p10 = dot(q1, k0, 1, 1).astype(BF16)
            p11 = jnp.where(lower, dot(q1, k1, 1, 1), 0.0).astype(BF16)
            probs[h, 0] = p00
            probs[h, 1] = p10
            probs[h, 2] = p11
            attn[lo, cols] = dot(p00, v0, 1, 0)
            attn[hi, cols] = dot(p10, v0, 1, 0) + dot(p11, v1, 1, 0)
            gain = gain_ref[pl.ds(h, 1), :]
            for t in range(4):
                rows = pl.ds(t * 128, 128)
                gate = jax.nn.sigmoid(g[rows, cols].astype(F32))
                sg[rows, cols] = gate
                w[rows, cols] = c[rows, cols].astype(F32) * gate * gain

    for part in range(PARTS):
        for src, dst, sem in pairs[2:]:
            load(src, dst, sem, part).wait()
    within_forward(0, 4)
    for part in range(PARTS):
        prefixes.add_up(part)
    for part in range(PARTS):
        prefixes.finish(part)
        within_forward(4 + part, 5 + part)

    for part in range(PARTS):
        prefixes.arrived(part)
        heads = range(part * HH, (part + 1) * HH)
        for i, h in enumerate(heads):
            pb[h] = prefixes.state(part, i).astype(BF16)
        for t in range(4):
            rows = pl.ds(t * 128, 128)
            squares, products = acc_s[rows, :], acc_p[rows, :]
            for h in heads:
                cols = cols_of(h)
                a = attn[rows, cols] + dot(q[rows, cols], pb[h], 1, 0)
                attn[rows, cols] = a
                squares = squares + a * a
                products = products + a * w[rows, cols]
            if part < PARTS - 1:
                acc_s[rows, :] = squares
                acc_p[rows, :] = products
            else:
                st[pl.ds(t, 1), :] = jnp.sum(squares.T, axis=0, keepdims=True)
                st[pl.ds(4 + t, 1), :] = jnp.sum(products.T, axis=0, keepdims=True)

    for dy, dc in PEERS:
        remote(st, st_r.at[tp], t_s.at[0], t_r.at[0], (me, peer(dy, dc))).start()

    st_r[tp] = st[...]
    peers = st_r.at[pl.ds(0, TP - 1)]
    peers_copy = remote(peers, peers, t_s.at[0], t_r.at[0], (me, lax.rem(tp + 1, TP)))
    peers_copy.wait_recv()
    sums = jnp.sum(st_r[...], axis=0)
    feat = float(HEADS * WIDTH)
    rinv = lax.rsqrt(sums[0:4] / feat + 1e-06)
    mean = sums[4:8] * rinv / feat
    for t in range(4):
        rows = pl.ds(t * 128, 128)
        rinv_c[rows, :] = jnp.broadcast_to(rinv[t : t + 1], (128, 128)).T
        pm_c[rows, :] = jnp.broadcast_to(mean[t : t + 1], (128, 128)).T

    for part in range(PARTS):
        for h in range(part * HH, (part + 1) * HH):
            cols = cols_of(h)
            for t in range(4):
                rows = pl.ds(t * 128, 128)
                ri = rinv_c[rows, :]
                xhat = attn[rows, cols] * ri
                d[rows, cols] = (ri * (w[rows, cols] - xhat * pm_c[rows, :])).astype(BF16)
            l_b[cols, :] = dot(q[:, cols], d[:, cols], 0, 0)

        suffixes.send(part)

    @pl.loop(0, HD)
    def _(h):
        cols = cols_of(h)
        gain = gain_ref[pl.ds(h, 1), :]
        part = jnp.zeros((8, WIDTH), F32)
        for t in range(4):
            rows = pl.ds(t * 128, 128)
            xhat = attn[rows, cols] * rinv_c[rows, :]
            normed = xhat * gain
            gate = sg[rows, cols]
            cot = c[rows, cols].astype(F32)
            o_gated[rows, cols] = (normed * gate).astype(BF16)
            o_gg[rows, cols] = (cot * normed * gate * (1.0 - gate)).astype(BF16)
            part = part + jnp.sum((cot * gate * xhat).reshape(16, 8, WIDTH), axis=0)
        gs[pl.ds(h, 1), :] = jnp.sum(part, axis=0, keepdims=True)

    @pl.loop(1, NX)
    def _(i):
        to = lax.rem(x + i, NX) * NZ + z
        remote(gs, gx_r.at[x], x_s.at[0], x_r.at[0], (to, tp)).start()

    gx_r[x] = gs[...]
    xs = gx_r.at[pl.ds(0, NX - 1)]
    xs_copy = remote(xs, xs, x_s.at[0], x_r.at[0], (lax.rem(x + 1, NX) * NZ + z, tp))

    def within_backward(first, last):
        @pl.loop(first, last)
        def _(h):
            cols = cols_of(h)
            q0, q1 = q[lo, cols], q[hi, cols]
            k0, k1 = k[lo, cols], k[hi, cols]
            v0, v1 = v[lo, cols], v[hi, cols]
            d0, d1 = d[lo, cols], d[hi, cols]
            prefix = pb[h]
            s00 = jnp.where(lower, dot(d0, v0, 1, 1), 0.0).astype(BF16)
            s10 = dot(d1, v0, 1, 1).astype(BF16)
            s11 = jnp.where(lower, dot(d1, v1, 1, 1), 0.0).astype(BF16)
            o_dq[lo, cols] = (dot(s00, k0, 1, 0) + dot(d0, prefix, 1, 1)).astype(BF16)
            o_dq[hi, cols] = (dot(s10, k0, 1, 0) + dot(s11, k1, 1, 0) + dot(d1, prefix, 1, 1)).astype(BF16)
            dk[lo, cols] = dot(s00, q0, 0, 0) + dot(s10, q1, 0, 0)
            dk[hi, cols] = dot(s11, q1, 0, 0)
            dv[lo, cols] = dot(probs[h, 0], d0, 0, 0) + dot(probs[h, 1], d1, 0, 0)
            dv[hi, cols] = dot(probs[h, 2], d1, 0, 0)

    for part in range(PARTS):
        suffixes.add_up(part)
        if part < PARTS - 1:
            within_backward(part, part + 1)
    xs_copy.wait_recv()
    gz[...] = jnp.sum(gx_r[...], axis=0)

    @pl.loop(1, NZ)
    def _(i):
        to = x * NZ + lax.rem(z + i, NZ)
        remote(gz, gz_r.at[z], z_s.at[0], z_r.at[0], (to, tp)).start()

    gz_r[z] = gz[...]
    for part in range(PARTS):
        suffixes.finish(part)
        within_backward(PARTS - 1 + part, PARTS + part)
    within_backward(2 * PARTS - 1, HD)

    for part in range(PARTS):
        suffixes.arrived(part)

        for i in range(HH):
            cols = cols_of(part * HH + i)
            suffix = suffixes.state(part, i).astype(BF16)
            o_dk[:, cols] = (dk[:, cols] + dot(v[:, cols], suffix, 1, 1)).astype(BF16)
            o_dv[:, cols] = (dv[:, cols] + dot(k[:, cols], suffix, 1, 0)).astype(BF16)

    zs = gz_r.at[pl.ds(0, NZ - 1)]
    zs_copy = remote(zs, zs, z_s.at[0], z_r.at[0], (x * NZ + lax.rem(z + 1, NZ), tp))
    zs_copy.wait_recv()
    gain_out[...] = jnp.sum(gz_r[...], axis=0)

    prefixes.sent()
    suffixes.sent()
    peers_copy.wait_send()
    xs_copy.wait_send()
    zs_copy.wait_send()


def store(*refs):
    n = len(refs) // 2
    sem = refs[-1]
    srcs, dsts = refs[:n], refs[n:2 * n]

    def parts(start):
        for i, (src, dst) in enumerate(zip(srcs, dsts)):
            if src.shape[0] == TOK:
                for half in range(HALVES):
                    rows = pl.ds(half * HALF_TOK, HALF_TOK)
                    start(pltpu.make_async_copy(src.at[rows], dst.at[rows], sem.at[i, half]))
            else:
                start(pltpu.make_async_copy(src, dst, sem.at[i, 0]))

    parts(lambda copy: copy.start())
    parts(lambda copy: copy.wait())


def body(query, key_in, value, gate, gain, grad_out):
    any_space = pl.BlockSpec(memory_space=pl.ANY)
    vmem = pl.BlockSpec(memory_space=pltpu.VMEM)
    big = jax.ShapeDtypeStruct((TOK, FEAT_DEV), BF16)
    narrow = pltpu.VMEM((TOK, FEAT_DEV), BF16)
    wide = pltpu.VMEM((TOK, FEAT_DEV), F32)
    states = pltpu.VMEM((HD * WIDTH, WIDTH), F32)
    pieces = pltpu.VMEM((PARTS, GROUP, PIECE, WIDTH), F32)
    totals = pltpu.VMEM((PARTS, GROUP + 1, PIECE, WIDTH), F32)
    sums = pltpu.VMEM((PARTS, NX, PIECE, WIDTH), F32)
    column = pltpu.VMEM((TOK, WIDTH), F32)
    tile = pltpu.VMEM((8, WIDTH), F32)
    each = pltpu.SemaphoreType.DMA((PARTS,))
    one = pltpu.SemaphoreType.DMA((1,))
    scratch = (
        [narrow] * 5
        + [wide] * 5
        + [pltpu.VMEM((HD, 3, HALF_TOK, HALF_TOK), BF16), narrow, pltpu.VMEM((HD, WIDTH, WIDTH), BF16)]
        + [states, pieces, totals, pieces, sums, sums] * 2
        + [column] * 4
        + [tile, pltpu.VMEM((TP, 8, WIDTH), F32)]
        + [tile, pltpu.VMEM((NX, 8, WIDTH), F32), tile, pltpu.VMEM((NZ, 8, WIDTH), F32)]
        + [tile, one, pltpu.SemaphoreType.DMA((5, PARTS))]
        + [one] * 6
        + [each] * 12
    )
    outs = pl.pallas_call(
        kernel,
        out_shape=[narrow] * 5 + [tile],
        in_specs=[any_space] * 6,
        out_specs=[vmem] * 6,
        scratch_shapes=scratch,
        compiler_params=pltpu.CompilerParams(
            collective_id=0, has_side_effects=True, vmem_limit_bytes=56 * 2**20
        ),
        name="lightning",
    )(query, key_in, value, gate, grad_out, gain.reshape(8, WIDTH))
    gated, dq, dk, dv, gg, gain_gradient = pl.pallas_call(
        store,
        out_shape=[big] * 5 + [jax.ShapeDtypeStruct((8, WIDTH), F32)],
        in_specs=[any_space] * 6,
        out_specs=[any_space] * 6,
        scratch_shapes=[pltpu.SemaphoreType.DMA((6, HALVES))],
        compiler_params=pltpu.CompilerParams(vmem_limit_bytes=4 * 2**20),
        name="store",
    )(*outs)
    return gated, dq, dk, dv, gg, gain_gradient.reshape(-1)


def solution(mesh):
    block = P("ctx", "tp")
    specs = (block, block, block, block, P("tp"), block)
    out_specs = (block, block, block, block, block, P("tp"))
    return jax.shard_map(body, mesh=mesh, in_specs=specs, out_specs=out_specs, check_vma=False)
```

```python
import functools

import jax
import jax.numpy as jnp
from jax import lax
from jax.experimental import pallas as pl
from jax.experimental.pallas import tpu as pltpu
from jax.sharding import PartitionSpec as P

HEADS = 64
WIDTH = 128
MESH = pl.DeviceIdType.MESH
F32 = jnp.float32
BF16 = jnp.bfloat16
NX, NZ = 4, 8
CTX = NX * NZ
TP = 8
TOK = 512
HD = 8
FEAT_DEV = HD * WIDTH
PARTS = 4
HH = HD // PARTS
FAR_FIRST = (2, 1, 3, 0)
REACH = [(dx, dz) for dx in FAR_FIRST for dz in (2, 6, 1, 7, 0) if dx or dz] + [(0, 4), (0, 3), (0, 5)]
PEERS = [(2, 1), (2, 0), (1, 1), (3, 1), (1, 0), (3, 0), (0, 1)]
GROUP = 16
PIECE = HH * WIDTH // GROUP
HALF_TOK = TOK // 2


def dot(a, b, ca, cb):
    return lax.dot_general(a, b, (((ca,), (cb,)), ((), ())), preferred_element_type=F32)


def kernel(
    q_in, k_in, v_in, g_in, c_in, gain_in,
    o_gated, o_dq, o_dk, o_dv, o_gg, gain_out,
    q, k, v, g, c,
    sg, w, attn, dk, dv, probs, d, pb,
    l_a, r_a, p_a, s_a, e_a, er_a, l_b, r_b, p_b, s_b, e_b, er_b,
    acc_s, acc_p, rinv_c, pm_c, st, st_r, gs, gx_r, gz, gz_r,
    gain_ref, gain_sem, in_sem,
    t_s, t_r, x_s, x_r, z_s, z_r,
    *sems,
):
    sems_a, sems_b = sems[:6], sems[6:]
    me = lax.axis_index("ctx")
    tp = lax.axis_index("tp")
    x, z = me // NZ, lax.rem(me, NZ)

    def peer(dy, dc):
        return lax.rem(tp // 2 + dy, TP // 2) * 2 + lax.rem(lax.rem(tp, 2) + dc, 2)

    def load(src, dst, sem, part):
        cols = pl.ds(part * HH * WIDTH, HH * WIDTH)
        return pltpu.make_async_copy(src.at[:, cols], dst.at[:, cols], in_sem.at[sem, part])

    pairs = ((k_in, k, 0), (v_in, v, 1), (q_in, q, 2), (g_in, g, 3), (c_in, c, 4))
    barrier = pltpu.get_barrier_semaphore()
    for dx, dz in REACH:
        to = lax.rem(x + dx, NX) * NZ + lax.rem(z + dz, NZ)
        pl.semaphore_signal(barrier, inc=1, device_id=(to, tp), device_id_type=MESH)
    for dy, dc in PEERS:
        pl.semaphore_signal(barrier, inc=1, device_id=(me, peer(dy, dc)), device_id_type=MESH)

    for part in range(PARTS):
        for src, dst, sem in pairs[:2]:
            load(src, dst, sem, part).start()

    for part in range(PARTS):
        for src, dst, sem in pairs[2:]:
            load(src, dst, sem, part).start()
    gain_load = pltpu.make_async_copy(gain_in, gain_ref, gain_sem.at[0])
    gain_load.start()

    def remote(src, dst, ss, rs, to):
        return pltpu.make_async_remote_copy(
            src_ref=src, dst_ref=dst, send_sem=ss, recv_sem=rs, device_id=to, device_id_type=MESH
        )

    class Sum:
        def __init__(self, reverse, l, r, p, s, e, e_r, s1, r1, s2, r2, s3, r3):
            self.rx = NX - 1 - x if reverse else x
            self.rz = NZ - 1 - z if reverse else z
            self.reverse = reverse
            self.l, self.r, self.p, self.s, self.e, self.e_r = l, r, p, s, e, e_r
            self.up, self.across, self.down = (s1, r1), (s2, r2), (s3, r3)

        def device(self, rx, rz):
            ctx = rx * NZ + rz
            return (CTX - 1 - ctx if self.reverse else ctx, tp)

        def some(self, buf, sems, part):
            most = buf.at[part, pl.ds(0, GROUP - 1)]
            return remote(most, most, sems[0].at[part], sems[1].at[part], (lax.rem(me + 1, CTX), tp))

        def order(self, turn):
            u = lax.rem(self.rz - turn + NZ, NZ)
            second, place = u // 4, lax.rem(u, 4)
            outer = (place == 0) | (place == 3)
            low = (place < 2) == (second == 0)
            far = jnp.where(outer, jnp.where(low, 0, 1), jnp.where((lax.rem(u - 2 + NZ, NZ) < 4) == (lax.rem(u - 2 + NZ, 4) < 2), 2, 3))
            inner_second, inner_place = lax.rem(u - 2 + NZ, NZ) // 4, lax.rem(u - 2 + NZ, 4)
            stay = jnp.where(
                outer,
                jnp.where((inner_place == 2) == (inner_second == 0), 2, 3),
                jnp.where((place == 2) == (second == 0), 0, 1),
            )
            return far, (far + 1 - 2 * lax.rem(far, 2), stay + 1 - 2 * lax.rem(stay, 2), stay)

        def home(self, part, kind):
            turn = part % 2 + 2 * (kind // 2)
            second = lax.rem(self.rz - turn + NZ, NZ) // 4
            start = lax.rem(turn + 4 * second, NZ)
            off = jnp.where(lax.rem(kind, 2) == second, 2, 1)
            ahead = jnp.maximum(start - 4, 0)
            place = jnp.where(self.rz < ahead, self.rz, self.rz - start + ahead)
            return lax.rem(start + off, NZ), place

        def role(self, part):
            turn = part % 2
            u = lax.rem(self.rz - turn + NZ, NZ)
            outer_a, outer_b, inner_a = (u == 2) | (u == 5), (u == 1) | (u == 6), (u == 4) | (u == 7)
            kind = jnp.where(outer_a, 0, jnp.where(outer_b, 1, jnp.where(inner_a, 2, 3)))
            partner = jnp.where(kind < 2, 7 - u, jnp.where(kind == 2, 11 - u, 3 - u))
            base = jnp.where((u == 1) | (u == 2), 0, jnp.where((u == 5) | (u == 6), 4, jnp.where((u == 3) | (u == 4), 2, 6)))
            start = lax.rem(base + turn, NZ)
            return kind, lax.rem(partner + turn, NZ), start, jnp.maximum(start - 4, 0)

        def send(self, part):
            first = part * HH * WIDTH
            turn = part % 2
            far, near = self.order(turn)
            homes = [(kind, *self.home(part, kind)) for kind in (far, *near)]
            for i in FAR_FIRST:
                hx = lax.rem(self.rx + i, NX)
                for kind, hz, place in homes:
                    rows = pl.ds(pl.multiple_of(first + (kind * NX + hx) * PIECE, PIECE), PIECE)
                    slot = self.rx * 4 + place

                    def go():
                        remote(
                            self.l.at[rows], self.r.at[part, slot], self.up[0].at[part], self.up[1].at[part],
                            self.device(hx, hz),
                        ).start()

                    if i:
                        go()
                    else:
                        pl.when(hz != self.rz)(go)

                        @pl.when(hz == self.rz)
                        def _():
                            self.r[part, slot] = self.l[rows, :]

        def across_copy(self, part, partner):
            return remote(
                self.e.at[part], self.e_r.at[part], self.across[0].at[part], self.across[1].at[part],
                self.device(self.rx, partner),
            )

        def add_up(self, part):
            _, partner, start, ahead = self.role(part)
            self.some(self.r, self.up, part).wait_recv()
            total = jnp.zeros((PIECE, WIDTH), F32)
            for slot in range(GROUP):
                self.p[part, slot] = total
                total = total + self.r[part, slot]
            self.p[part, GROUP] = total
            cut = jnp.where(start < 4, 4, ahead)
            for row in range(NX):
                self.e[part, row] = self.p[part, row * 4 + cut]
            self.across_copy(part, partner).start()

        def finish(self, part):
            kind, partner, start, ahead = self.role(part)
            self.across_copy(part, partner).wait_recv()
            for row in range(NX):
                whole = self.e_r[part, row]
                earlier = self.e_r[part, row - 1] if row else jnp.zeros((PIECE, WIDTH), F32)
                for m in range(4):
                    self.p[part, row * 4 + m] += jnp.where(m < ahead, earlier, whole)
            slot = kind * NX + self.rx
            off = lax.rem(self.rz - start + NZ, NZ)
            for i in FAR_FIRST:
                row = lax.rem(self.rx + i, NX)
                for step in (3, 0, 2, 1):
                    to_z = lax.rem(start + jnp.where(off == 1, step, 3 - step), NZ)
                    m = jnp.where(to_z < ahead, to_z, to_z - start + ahead)
                    done = self.p.at[part, row * 4 + m]

                    def go():
                        remote(
                            done, self.s.at[part, slot], self.down[0].at[part], self.down[1].at[part],
                            self.device(row, to_z),
                        ).start()

                    if i:
                        go()
                    else:
                        pl.when(to_z != self.rz)(go)

                        @pl.when(to_z == self.rz)
                        def _():
                            self.s[part, slot] = self.p[part, row * 4 + m]

        def arrived(self, part):
            self.some(self.s, self.down, part).wait_recv()

        def state(self, part, i):
            whole = WIDTH // PIECE
            return self.s[part, i * whole : (i + 1) * whole].reshape(WIDTH, WIDTH)

        def sent(self):
            for part in range(PARTS):
                self.some(self.r, self.up, part).wait_send()
                self.across_copy(part, 0).wait_send()
                self.some(self.s, self.down, part).wait_send()

    prefixes = Sum(False, l_a, r_a, p_a, s_a, e_a, er_a, *sems_a)
    suffixes = Sum(True, l_b, r_b, p_b, s_b, e_b, er_b, *sems_b)

    def cols_of(h):
        return pl.ds(h * WIDTH if isinstance(h, int) else pl.multiple_of(h * WIDTH, WIDTH), WIDTH)

    for part in range(PARTS):
        for src, dst, sem in pairs[:2]:
            load(src, dst, sem, part).wait()

        for h in range(part * HH, (part + 1) * HH):
            cols = cols_of(h)
            l_a[cols, :] = dot(k[:, cols], v[:, cols], 0, 0)

        if part == 0:
            pl.semaphore_wait(barrier, len(REACH) + len(PEERS))
        prefixes.send(part)

    lower = lax.broadcasted_iota(jnp.int32, (HALF_TOK, HALF_TOK), 0) >= lax.broadcasted_iota(
        jnp.int32, (HALF_TOK, HALF_TOK), 1
    )
    lo, hi = pl.ds(0, HALF_TOK), pl.ds(HALF_TOK, HALF_TOK)

    gain_load.wait()
    acc_s[...] = jnp.zeros_like(acc_s)
    acc_p[...] = jnp.zeros_like(acc_p)

    def within_forward(first, last):
        @pl.loop(first, last)
        def _(h):
            cols = cols_of(h)
            q0, q1 = q[lo, cols], q[hi, cols]
            k0, k1 = k[lo, cols], k[hi, cols]
            v0, v1 = v[lo, cols], v[hi, cols]
            p00 = jnp.where(lower, dot(q0, k0, 1, 1), 0.0).astype(BF16)
            p10 = dot(q1, k0, 1, 1).astype(BF16)
            p11 = jnp.where(lower, dot(q1, k1, 1, 1), 0.0).astype(BF16)
            probs[h, 0] = p00
            probs[h, 1] = p10
            probs[h, 2] = p11
            attn[lo, cols] = dot(p00, v0, 1, 0)
            attn[hi, cols] = dot(p10, v0, 1, 0) + dot(p11, v1, 1, 0)
            gain = gain_ref[pl.ds(h, 1), :]
            for t in range(4):
                rows = pl.ds(t * 128, 128)
                gate = jax.nn.sigmoid(g[rows, cols].astype(F32))
                sg[rows, cols] = gate
                w[rows, cols] = c[rows, cols].astype(F32) * gate * gain

    for part in range(PARTS):
        for src, dst, sem in pairs[2:]:
            load(src, dst, sem, part).wait()
    within_forward(0, 4)
    for part in range(PARTS):
        prefixes.add_up(part)
    for part in range(PARTS):
        prefixes.finish(part)
        within_forward(4 + part, 5 + part)

    for part in range(PARTS):
        prefixes.arrived(part)
        heads = range(part * HH, (part + 1) * HH)
        for i, h in enumerate(heads):
            pb[h] = prefixes.state(part, i).astype(BF16)
        for t in range(4):
            rows = pl.ds(t * 128, 128)
            squares, products = acc_s[rows, :], acc_p[rows, :]
            for h in heads:
                cols = cols_of(h)
                a = attn[rows, cols] + dot(q[rows, cols], pb[h], 1, 0)
                attn[rows, cols] = a
                squares = squares + a * a
                products = products + a * w[rows, cols]
            if part < PARTS - 1:
                acc_s[rows, :] = squares
                acc_p[rows, :] = products
            else:
                st[pl.ds(t, 1), :] = jnp.sum(squares.T, axis=0, keepdims=True)
                st[pl.ds(4 + t, 1), :] = jnp.sum(products.T, axis=0, keepdims=True)

    for dy, dc in PEERS:
        remote(st, st_r.at[tp], t_s.at[0], t_r.at[0], (me, peer(dy, dc))).start()

    st_r[tp] = st[...]
    peers = st_r.at[pl.ds(0, TP - 1)]
    peers_copy = remote(peers, peers, t_s.at[0], t_r.at[0], (me, lax.rem(tp + 1, TP)))
    peers_copy.wait_recv()
    sums = jnp.sum(st_r[...], axis=0)
    feat = float(HEADS * WIDTH)
    rinv = lax.rsqrt(sums[0:4] / feat + 1e-06)
    mean = sums[4:8] * rinv / feat
    for t in range(4):
        rows = pl.ds(t * 128, 128)
        rinv_c[rows, :] = jnp.broadcast_to(rinv[t : t + 1], (128, 128)).T
        pm_c[rows, :] = jnp.broadcast_to(mean[t : t + 1], (128, 128)).T

    for part in range(PARTS):
        for h in range(part * HH, (part + 1) * HH):
            cols = cols_of(h)
            for t in range(4):
                rows = pl.ds(t * 128, 128)
                ri = rinv_c[rows, :]
                xhat = attn[rows, cols] * ri
                d[rows, cols] = (ri * (w[rows, cols] - xhat * pm_c[rows, :])).astype(BF16)
            l_b[cols, :] = dot(q[:, cols], d[:, cols], 0, 0)

        suffixes.send(part)

    @pl.loop(0, HD)
    def _(h):
        cols = cols_of(h)
        gain = gain_ref[pl.ds(h, 1), :]
        part = jnp.zeros((8, WIDTH), F32)
        for t in range(4):
            rows = pl.ds(t * 128, 128)
            xhat = attn[rows, cols] * rinv_c[rows, :]
            normed = xhat * gain
            gate = sg[rows, cols]
            cot = c[rows, cols].astype(F32)
            o_gated[rows, cols] = (normed * gate).astype(BF16)
            o_gg[rows, cols] = (cot * normed * gate * (1.0 - gate)).astype(BF16)
            part = part + jnp.sum((cot * gate * xhat).reshape(16, 8, WIDTH), axis=0)
        gs[pl.ds(h, 1), :] = jnp.sum(part, axis=0, keepdims=True)

    @pl.loop(1, NX)
    def _(i):
        to = lax.rem(x + i, NX) * NZ + z
        remote(gs, gx_r.at[x], x_s.at[0], x_r.at[0], (to, tp)).start()

    gx_r[x] = gs[...]
    xs = gx_r.at[pl.ds(0, NX - 1)]
    xs_copy = remote(xs, xs, x_s.at[0], x_r.at[0], (lax.rem(x + 1, NX) * NZ + z, tp))

    def within_backward(first, last):
        @pl.loop(first, last)
        def _(h):
            cols = cols_of(h)
            q0, q1 = q[lo, cols], q[hi, cols]
            k0, k1 = k[lo, cols], k[hi, cols]
            v0, v1 = v[lo, cols], v[hi, cols]
            d0, d1 = d[lo, cols], d[hi, cols]
            prefix = pb[h]
            s00 = jnp.where(lower, dot(d0, v0, 1, 1), 0.0).astype(BF16)
            s10 = dot(d1, v0, 1, 1).astype(BF16)
            s11 = jnp.where(lower, dot(d1, v1, 1, 1), 0.0).astype(BF16)
            o_dq[lo, cols] = (dot(s00, k0, 1, 0) + dot(d0, prefix, 1, 1)).astype(BF16)
            o_dq[hi, cols] = (dot(s10, k0, 1, 0) + dot(s11, k1, 1, 0) + dot(d1, prefix, 1, 1)).astype(BF16)
            dk[lo, cols] = dot(s00, q0, 0, 0) + dot(s10, q1, 0, 0)
            dk[hi, cols] = dot(s11, q1, 0, 0)
            dv[lo, cols] = dot(probs[h, 0], d0, 0, 0) + dot(probs[h, 1], d1, 0, 0)
            dv[hi, cols] = dot(probs[h, 2], d1, 0, 0)

    for part in range(PARTS):
        suffixes.add_up(part)
        if part < PARTS - 1:
            within_backward(part, part + 1)
    xs_copy.wait_recv()
    gz[...] = jnp.sum(gx_r[...], axis=0)

    @pl.loop(1, NZ)
    def _(i):
        to = x * NZ + lax.rem(z + i, NZ)
        remote(gz, gz_r.at[z], z_s.at[0], z_r.at[0], (to, tp)).start()

    gz_r[z] = gz[...]
    for part in range(PARTS):
        suffixes.finish(part)
        within_backward(PARTS - 1 + part, PARTS + part)
    within_backward(2 * PARTS - 1, HD)

    for part in range(PARTS):
        suffixes.arrived(part)

        for i in range(HH):
            cols = cols_of(part * HH + i)
            suffix = suffixes.state(part, i).astype(BF16)
            o_dk[:, cols] = (dk[:, cols] + dot(v[:, cols], suffix, 1, 1)).astype(BF16)
            o_dv[:, cols] = (dv[:, cols] + dot(k[:, cols], suffix, 1, 0)).astype(BF16)

    zs = gz_r.at[pl.ds(0, NZ - 1)]
    zs_copy = remote(zs, zs, z_s.at[0], z_r.at[0], (x * NZ + lax.rem(z + 1, NZ), tp))
    zs_copy.wait_recv()
    gain_out[...] = jnp.sum(gz_r[...], axis=0)

    prefixes.sent()
    suffixes.sent()
    peers_copy.wait_send()
    xs_copy.wait_send()
    zs_copy.wait_send()


def store(*refs):
    n = len(refs) // 2
    sem = refs[-1]
    srcs, dsts = refs[:n], refs[n:2 * n]

    def parts(start):
        for i, (src, dst) in enumerate(zip(srcs, dsts)):
            start(pltpu.make_async_copy(src, dst, sem.at[i]))

    parts(lambda copy: copy.start())
    parts(lambda copy: copy.wait())


def body(query, key_in, value, gate, gain, grad_out):
    any_space = pl.BlockSpec(memory_space=pl.ANY)
    vmem = pl.BlockSpec(memory_space=pltpu.VMEM)
    big = jax.ShapeDtypeStruct((TOK, FEAT_DEV), BF16)
    narrow = pltpu.VMEM((TOK, FEAT_DEV), BF16)
    wide = pltpu.VMEM((TOK, FEAT_DEV), F32)
    states = pltpu.VMEM((HD * WIDTH, WIDTH), F32)
    pieces = pltpu.VMEM((PARTS, GROUP, PIECE, WIDTH), F32)
    totals = pltpu.VMEM((PARTS, GROUP + 1, PIECE, WIDTH), F32)
    sums = pltpu.VMEM((PARTS, NX, PIECE, WIDTH), F32)
    column = pltpu.VMEM((TOK, WIDTH), F32)
    tile = pltpu.VMEM((8, WIDTH), F32)
    each = pltpu.SemaphoreType.DMA((PARTS,))
    one = pltpu.SemaphoreType.DMA((1,))
    scratch = (
        [narrow] * 5
        + [wide] * 5
        + [pltpu.VMEM((HD, 3, HALF_TOK, HALF_TOK), BF16), narrow, pltpu.VMEM((HD, WIDTH, WIDTH), BF16)]
        + [states, pieces, totals, pieces, sums, sums] * 2
        + [column] * 4
        + [tile, pltpu.VMEM((TP, 8, WIDTH), F32)]
        + [tile, pltpu.VMEM((NX, 8, WIDTH), F32), tile, pltpu.VMEM((NZ, 8, WIDTH), F32)]
        + [tile, one, pltpu.SemaphoreType.DMA((5, PARTS))]
        + [one] * 6
        + [each] * 12
    )
    outs = pl.pallas_call(
        kernel,
        out_shape=[narrow] * 5 + [tile],
        in_specs=[any_space] * 6,
        out_specs=[vmem] * 6,
        scratch_shapes=scratch,
        compiler_params=pltpu.CompilerParams(
            collective_id=0, has_side_effects=True, vmem_limit_bytes=56 * 2**20
        ),
        name="lightning",
    )(query, key_in, value, gate, grad_out, gain.reshape(8, WIDTH))
    gated, dq, dk, dv, gg, gain_gradient = pl.pallas_call(
        store,
        out_shape=[big] * 5 + [jax.ShapeDtypeStruct((8, WIDTH), F32)],
        in_specs=[any_space] * 6,
        out_specs=[any_space] * 6,
        scratch_shapes=[pltpu.SemaphoreType.DMA((6,))],
        compiler_params=pltpu.CompilerParams(vmem_limit_bytes=4 * 2**20),
        name="store",
    )(*outs)
    return gated, dq, dk, dv, gg, gain_gradient.reshape(-1)


def solution(mesh):
    block = P("ctx", "tp")
    specs = (block, block, block, block, P("tp"), block)
    out_specs = (block, block, block, block, block, P("tp"))
    return jax.shard_map(body, mesh=mesh, in_specs=specs, out_specs=out_specs, check_vma=False)
```

```python
import functools

import jax
import jax.numpy as jnp
from jax import lax
from jax.experimental import pallas as pl
from jax.experimental.pallas import tpu as pltpu
from jax.sharding import PartitionSpec as P

HEADS = 64
WIDTH = 128
MESH = pl.DeviceIdType.MESH
F32 = jnp.float32
BF16 = jnp.bfloat16
NX, NZ = 4, 8
CTX = NX * NZ
TP = 8
TOK = 512
HD = 8
FEAT_DEV = HD * WIDTH
PARTS = 4
HH = HD // PARTS
FAR_FIRST = (2, 1, 3, 0)
REACH = [(dx, dz) for dx in FAR_FIRST for dz in (2, 6, 1, 7, 0) if dx or dz] + [(0, 4), (0, 3), (0, 5)]
PEERS = [(2, 1), (2, 0), (1, 1), (3, 1), (1, 0), (3, 0), (0, 1)]
GROUP = 16
PIECE = HH * WIDTH // GROUP
HALF_TOK = TOK // 2


def dot(a, b, ca, cb):
    return lax.dot_general(a, b, (((ca,), (cb,)), ((), ())), preferred_element_type=F32)


def kernel(
    q_in, k_in, v_in, g_in, c_in, gain_in,
    o_gated, o_dq, o_dk, o_dv, o_gg, gain_out,
    q, k, v, g, c,
    sg, w, attn, dk, dv, probs, d, pb,
    l_a, r_a, p_a, s_a, e_a, er_a, l_b, r_b, p_b, s_b, e_b, er_b,
    acc_s, acc_p, rinv_c, pm_c, st, st_r, gs, gx_r, gz, gz_r,
    gain_ref, gain_sem, in_sem,
    t_s, t_r, x_s, x_r, z_s, z_r,
    *sems,
):
    sems_a, sems_b = sems[:6], sems[6:]
    me = lax.axis_index("ctx")
    tp = lax.axis_index("tp")
    x, z = me // NZ, lax.rem(me, NZ)

    def peer(dy, dc):
        return lax.rem(tp // 2 + dy, TP // 2) * 2 + lax.rem(lax.rem(tp, 2) + dc, 2)

    def load(src, dst, sem, part):
        cols = pl.ds(part * HH * WIDTH, HH * WIDTH)
        return pltpu.make_async_copy(src.at[:, cols], dst.at[:, cols], in_sem.at[sem, part])

    pairs = ((k_in, k, 0), (v_in, v, 1), (q_in, q, 2), (g_in, g, 3), (c_in, c, 4))
    barrier = pltpu.get_barrier_semaphore()
    for dx, dz in REACH:
        to = lax.rem(x + dx, NX) * NZ + lax.rem(z + dz, NZ)
        pl.semaphore_signal(barrier, inc=1, device_id=(to, tp), device_id_type=MESH)
    for dy, dc in PEERS:
        pl.semaphore_signal(barrier, inc=1, device_id=(me, peer(dy, dc)), device_id_type=MESH)

    for part in range(PARTS):
        for src, dst, sem in pairs[:2]:
            load(src, dst, sem, part).start()

    for part in range(PARTS):
        for src, dst, sem in pairs[2:]:
            load(src, dst, sem, part).start()
    gain_load = pltpu.make_async_copy(gain_in, gain_ref, gain_sem.at[0])
    gain_load.start()

    def remote(src, dst, ss, rs, to):
        return pltpu.make_async_remote_copy(
            src_ref=src, dst_ref=dst, send_sem=ss, recv_sem=rs, device_id=to, device_id_type=MESH
        )

    class Sum:
        def __init__(self, reverse, l, r, p, s, e, e_r, s1, r1, s2, r2, s3, r3):
            self.rx = NX - 1 - x if reverse else x
            self.rz = NZ - 1 - z if reverse else z
            self.reverse = reverse
            self.l, self.r, self.p, self.s, self.e, self.e_r = l, r, p, s, e, e_r
            self.up, self.across, self.down = (s1, r1), (s2, r2), (s3, r3)

        def device(self, rx, rz):
            ctx = rx * NZ + rz
            return (CTX - 1 - ctx if self.reverse else ctx, tp)

        def some(self, buf, sems, part):
            most = buf.at[part, pl.ds(0, GROUP - 1)]
            return remote(most, most, sems[0].at[part], sems[1].at[part], (lax.rem(me + 1, CTX), tp))

        def order(self, turn):
            u = lax.rem(self.rz - turn + NZ, NZ)
            second, place = u // 4, lax.rem(u, 4)
            outer = (place == 0) | (place == 3)
            low = (place < 2) == (second == 0)
            far = jnp.where(outer, jnp.where(low, 0, 1), jnp.where((lax.rem(u - 2 + NZ, NZ) < 4) == (lax.rem(u - 2 + NZ, 4) < 2), 2, 3))
            inner_second, inner_place = lax.rem(u - 2 + NZ, NZ) // 4, lax.rem(u - 2 + NZ, 4)
            stay = jnp.where(
                outer,
                jnp.where((inner_place == 2) == (inner_second == 0), 2, 3),
                jnp.where((place == 2) == (second == 0), 0, 1),
            )
            return far, (far + 1 - 2 * lax.rem(far, 2), stay + 1 - 2 * lax.rem(stay, 2), stay)

        def home(self, part, kind):
            turn = part % 2 + 2 * (kind // 2)
            second = lax.rem(self.rz - turn + NZ, NZ) // 4
            start = lax.rem(turn + 4 * second, NZ)
            off = jnp.where(lax.rem(kind, 2) == second, 2, 1)
            ahead = jnp.maximum(start - 4, 0)
            place = jnp.where(self.rz < ahead, self.rz, self.rz - start + ahead)
            return lax.rem(start + off, NZ), place

        def role(self, part):
            turn = part % 2
            u = lax.rem(self.rz - turn + NZ, NZ)
            outer_a, outer_b, inner_a = (u == 2) | (u == 5), (u == 1) | (u == 6), (u == 4) | (u == 7)
            kind = jnp.where(outer_a, 0, jnp.where(outer_b, 1, jnp.where(inner_a, 2, 3)))
            partner = jnp.where(kind < 2, 7 - u, jnp.where(kind == 2, 11 - u, 3 - u))
            base = jnp.where((u == 1) | (u == 2), 0, jnp.where((u == 5) | (u == 6), 4, jnp.where((u == 3) | (u == 4), 2, 6)))
            start = lax.rem(base + turn, NZ)
            return kind, lax.rem(partner + turn, NZ), start, jnp.maximum(start - 4, 0)

        def send(self, part):
            first = part * HH * WIDTH
            turn = part % 2
            far, near = self.order(turn)
            homes = [(kind, *self.home(part, kind)) for kind in (far, *near)]
            for i in FAR_FIRST:
                hx = lax.rem(self.rx + i, NX)
                for kind, hz, place in homes:
                    rows = pl.ds(pl.multiple_of(first + (kind * NX + hx) * PIECE, PIECE), PIECE)
                    slot = self.rx * 4 + place

                    def go():
                        remote(
                            self.l.at[rows], self.r.at[part, slot], self.up[0].at[part], self.up[1].at[part],
                            self.device(hx, hz),
                        ).start()

                    if i:
                        go()
                    else:
                        pl.when(hz != self.rz)(go)

                        @pl.when(hz == self.rz)
                        def _():
                            self.r[part, slot] = self.l[rows, :]

        def across_copy(self, part, partner):
            return remote(
                self.e.at[part], self.e_r.at[part], self.across[0].at[part], self.across[1].at[part],
                self.device(self.rx, partner),
            )

        def add_up(self, part):
            _, partner, start, ahead = self.role(part)
            self.some(self.r, self.up, part).wait_recv()
            total = jnp.zeros((PIECE, WIDTH), F32)
            for slot in range(GROUP):
                self.p[part, slot] = total
                total = total + self.r[part, slot]
            self.p[part, GROUP] = total
            cut = jnp.where(start < 4, 4, ahead)
            for row in range(NX):
                self.e[part, row] = self.p[part, row * 4 + cut]
            self.across_copy(part, partner).start()

        def finish(self, part):
            kind, partner, start, ahead = self.role(part)
            self.across_copy(part, partner).wait_recv()
            slot = kind * NX + self.rx
            off = lax.rem(self.rz - start + NZ, NZ)
            for i in FAR_FIRST:
                row = lax.rem(self.rx + i, NX)
                whole = self.e_r[part, row]
                earlier = jnp.where(row > 0, self.e_r[part, jnp.maximum(row - 1, 0)], 0.0)
                for step in (3, 0, 2, 1):
                    to_z = lax.rem(start + jnp.where(off == 1, step, 3 - step), NZ)
                    m = jnp.where(to_z < ahead, to_z, to_z - start + ahead)
                    done = self.p.at[part, row * 4 + m]
                    done[...] += jnp.where(m < ahead, earlier, whole)

                    def go():
                        remote(
                            done, self.s.at[part, slot], self.down[0].at[part], self.down[1].at[part],
                            self.device(row, to_z),
                        ).start()

                    if i:
                        go()
                    else:
                        pl.when(to_z != self.rz)(go)

                        @pl.when(to_z == self.rz)
                        def _():
                            self.s[part, slot] = self.p[part, row * 4 + m]

        def arrived(self, part):
            self.some(self.s, self.down, part).wait_recv()

        def state(self, part, i):
            whole = WIDTH // PIECE
            return self.s[part, i * whole : (i + 1) * whole].reshape(WIDTH, WIDTH)

        def sent(self):
            for part in range(PARTS):
                self.some(self.r, self.up, part).wait_send()
                self.across_copy(part, 0).wait_send()
                self.some(self.s, self.down, part).wait_send()

    prefixes = Sum(False, l_a, r_a, p_a, s_a, e_a, er_a, *sems_a)
    suffixes = Sum(True, l_b, r_b, p_b, s_b, e_b, er_b, *sems_b)

    def cols_of(h):
        return pl.ds(h * WIDTH if isinstance(h, int) else pl.multiple_of(h * WIDTH, WIDTH), WIDTH)

    for part in range(PARTS):
        for src, dst, sem in pairs[:2]:
            load(src, dst, sem, part).wait()

        for h in range(part * HH, (part + 1) * HH):
            cols = cols_of(h)
            l_a[cols, :] = dot(k[:, cols], v[:, cols], 0, 0)

        if part == 0:
            pl.semaphore_wait(barrier, len(REACH) + len(PEERS))
        prefixes.send(part)

    lower = lax.broadcasted_iota(jnp.int32, (HALF_TOK, HALF_TOK), 0) >= lax.broadcasted_iota(
        jnp.int32, (HALF_TOK, HALF_TOK), 1
    )
    lo, hi = pl.ds(0, HALF_TOK), pl.ds(HALF_TOK, HALF_TOK)

    gain_load.wait()
    acc_s[...] = jnp.zeros_like(acc_s)
    acc_p[...] = jnp.zeros_like(acc_p)

    def within_forward(first, last):
        @pl.loop(first, last)
        def _(h):
            cols = cols_of(h)
            q0, q1 = q[lo, cols], q[hi, cols]
            k0, k1 = k[lo, cols], k[hi, cols]
            v0, v1 = v[lo, cols], v[hi, cols]
            p00 = jnp.where(lower, dot(q0, k0, 1, 1), 0.0).astype(BF16)
            p10 = dot(q1, k0, 1, 1).astype(BF16)
            p11 = jnp.where(lower, dot(q1, k1, 1, 1), 0.0).astype(BF16)
            probs[h, 0] = p00
            probs[h, 1] = p10
            probs[h, 2] = p11
            attn[lo, cols] = dot(p00, v0, 1, 0)
            attn[hi, cols] = dot(p10, v0, 1, 0) + dot(p11, v1, 1, 0)
            gain = gain_ref[pl.ds(h, 1), :]
            for t in range(4):
                rows = pl.ds(t * 128, 128)
                gate = jax.nn.sigmoid(g[rows, cols].astype(F32))
                sg[rows, cols] = gate
                w[rows, cols] = c[rows, cols].astype(F32) * gate * gain

    for part in range(PARTS):
        for src, dst, sem in pairs[2:]:
            load(src, dst, sem, part).wait()
    within_forward(0, 4)
    for part in range(PARTS):
        prefixes.add_up(part)
    for part in range(PARTS):
        prefixes.finish(part)
        within_forward(4 + part, 5 + part)

    for part in range(PARTS):
        prefixes.arrived(part)
        heads = range(part * HH, (part + 1) * HH)
        for i, h in enumerate(heads):
            pb[h] = prefixes.state(part, i).astype(BF16)
        for t in range(4):
            rows = pl.ds(t * 128, 128)
            squares, products = acc_s[rows, :], acc_p[rows, :]
            for h in heads:
                cols = cols_of(h)
                a = attn[rows, cols] + dot(q[rows, cols], pb[h], 1, 0)
                attn[rows, cols] = a
                squares = squares + a * a
                products = products + a * w[rows, cols]
            if part < PARTS - 1:
                acc_s[rows, :] = squares
                acc_p[rows, :] = products
            else:
                st[pl.ds(t, 1), :] = jnp.sum(squares.T, axis=0, keepdims=True)
                st[pl.ds(4 + t, 1), :] = jnp.sum(products.T, axis=0, keepdims=True)

    for dy, dc in PEERS:
        remote(st, st_r.at[tp], t_s.at[0], t_r.at[0], (me, peer(dy, dc))).start()

    st_r[tp] = st[...]
    peers = st_r.at[pl.ds(0, TP - 1)]
    peers_copy = remote(peers, peers, t_s.at[0], t_r.at[0], (me, lax.rem(tp + 1, TP)))
    peers_copy.wait_recv()
    sums = jnp.sum(st_r[...], axis=0)
    feat = float(HEADS * WIDTH)
    rinv = lax.rsqrt(sums[0:4] / feat + 1e-06)
    mean = sums[4:8] * rinv / feat
    for t in range(4):
        rows = pl.ds(t * 128, 128)
        rinv_c[rows, :] = jnp.broadcast_to(rinv[t : t + 1], (128, 128)).T
        pm_c[rows, :] = jnp.broadcast_to(mean[t : t + 1], (128, 128)).T

    for part in range(PARTS):
        for h in range(part * HH, (part + 1) * HH):
            cols = cols_of(h)
            for t in range(4):
                rows = pl.ds(t * 128, 128)
                ri = rinv_c[rows, :]
                xhat = attn[rows, cols] * ri
                d[rows, cols] = (ri * (w[rows, cols] - xhat * pm_c[rows, :])).astype(BF16)
            l_b[cols, :] = dot(q[:, cols], d[:, cols], 0, 0)

        suffixes.send(part)

    @pl.loop(0, HD)
    def _(h):
        cols = cols_of(h)
        gain = gain_ref[pl.ds(h, 1), :]
        part = jnp.zeros((8, WIDTH), F32)
        for t in range(4):
            rows = pl.ds(t * 128, 128)
            xhat = attn[rows, cols] * rinv_c[rows, :]
            normed = xhat * gain
            gate = sg[rows, cols]
            cot = c[rows, cols].astype(F32)
            o_gated[rows, cols] = (normed * gate).astype(BF16)
            o_gg[rows, cols] = (cot * normed * gate * (1.0 - gate)).astype(BF16)
            part = part + jnp.sum((cot * gate * xhat).reshape(16, 8, WIDTH), axis=0)
        gs[pl.ds(h, 1), :] = jnp.sum(part, axis=0, keepdims=True)

    @pl.loop(1, NX)
    def _(i):
        to = lax.rem(x + i, NX) * NZ + z
        remote(gs, gx_r.at[x], x_s.at[0], x_r.at[0], (to, tp)).start()

    gx_r[x] = gs[...]
    xs = gx_r.at[pl.ds(0, NX - 1)]
    xs_copy = remote(xs, xs, x_s.at[0], x_r.at[0], (lax.rem(x + 1, NX) * NZ + z, tp))

    def within_backward(first, last):
        @pl.loop(first, last)
        def _(h):
            cols = cols_of(h)
            q0, q1 = q[lo, cols], q[hi, cols]
            k0, k1 = k[lo, cols], k[hi, cols]
            v0, v1 = v[lo, cols], v[hi, cols]
            d0, d1 = d[lo, cols], d[hi, cols]
            prefix = pb[h]
            s00 = jnp.where(lower, dot(d0, v0, 1, 1), 0.0).astype(BF16)
            s10 = dot(d1, v0, 1, 1).astype(BF16)
            s11 = jnp.where(lower, dot(d1, v1, 1, 1), 0.0).astype(BF16)
            o_dq[lo, cols] = (dot(s00, k0, 1, 0) + dot(d0, prefix, 1, 1)).astype(BF16)
            o_dq[hi, cols] = (dot(s10, k0, 1, 0) + dot(s11, k1, 1, 0) + dot(d1, prefix, 1, 1)).astype(BF16)
            dk[lo, cols] = dot(s00, q0, 0, 0) + dot(s10, q1, 0, 0)
            dk[hi, cols] = dot(s11, q1, 0, 0)
            dv[lo, cols] = dot(probs[h, 0], d0, 0, 0) + dot(probs[h, 1], d1, 0, 0)
            dv[hi, cols] = dot(probs[h, 2], d1, 0, 0)

    for part in range(PARTS):
        suffixes.add_up(part)
        if part < PARTS - 1:
            within_backward(part, part + 1)
    xs_copy.wait_recv()
    gz[...] = jnp.sum(gx_r[...], axis=0)

    @pl.loop(1, NZ)
    def _(i):
        to = x * NZ + lax.rem(z + i, NZ)
        remote(gz, gz_r.at[z], z_s.at[0], z_r.at[0], (to, tp)).start()

    gz_r[z] = gz[...]
    for part in range(PARTS):
        suffixes.finish(part)
        within_backward(PARTS - 1 + part, PARTS + part)
    within_backward(2 * PARTS - 1, HD)

    for part in range(PARTS):
        suffixes.arrived(part)

        for i in range(HH):
            cols = cols_of(part * HH + i)
            suffix = suffixes.state(part, i).astype(BF16)
            o_dk[:, cols] = (dk[:, cols] + dot(v[:, cols], suffix, 1, 1)).astype(BF16)
            o_dv[:, cols] = (dv[:, cols] + dot(k[:, cols], suffix, 1, 0)).astype(BF16)

    zs = gz_r.at[pl.ds(0, NZ - 1)]
    zs_copy = remote(zs, zs, z_s.at[0], z_r.at[0], (x * NZ + lax.rem(z + 1, NZ), tp))
    zs_copy.wait_recv()
    gain_out[...] = jnp.sum(gz_r[...], axis=0)

    prefixes.sent()
    suffixes.sent()
    peers_copy.wait_send()
    xs_copy.wait_send()
    zs_copy.wait_send()


def store(*refs):
    n = len(refs) // 2
    sem = refs[-1]
    srcs, dsts = refs[:n], refs[n:2 * n]

    def parts(start):
        for i, (src, dst) in enumerate(zip(srcs, dsts)):
            start(pltpu.make_async_copy(src, dst, sem.at[i]))

    parts(lambda copy: copy.start())
    parts(lambda copy: copy.wait())


def body(query, key_in, value, gate, gain, grad_out):
    any_space = pl.BlockSpec(memory_space=pl.ANY)
    vmem = pl.BlockSpec(memory_space=pltpu.VMEM)
    big = jax.ShapeDtypeStruct((TOK, FEAT_DEV), BF16)
    narrow = pltpu.VMEM((TOK, FEAT_DEV), BF16)
    wide = pltpu.VMEM((TOK, FEAT_DEV), F32)
    states = pltpu.VMEM((HD * WIDTH, WIDTH), F32)
    pieces = pltpu.VMEM((PARTS, GROUP, PIECE, WIDTH), F32)
    totals = pltpu.VMEM((PARTS, GROUP + 1, PIECE, WIDTH), F32)
    sums = pltpu.VMEM((PARTS, NX, PIECE, WIDTH), F32)
    column = pltpu.VMEM((TOK, WIDTH), F32)
    tile = pltpu.VMEM((8, WIDTH), F32)
    each = pltpu.SemaphoreType.DMA((PARTS,))
    one = pltpu.SemaphoreType.DMA((1,))
    scratch = (
        [narrow] * 5
        + [wide] * 5
        + [pltpu.VMEM((HD, 3, HALF_TOK, HALF_TOK), BF16), narrow, pltpu.VMEM((HD, WIDTH, WIDTH), BF16)]
        + [states, pieces, totals, pieces, sums, sums] * 2
        + [column] * 4
        + [tile, pltpu.VMEM((TP, 8, WIDTH), F32)]
        + [tile, pltpu.VMEM((NX, 8, WIDTH), F32), tile, pltpu.VMEM((NZ, 8, WIDTH), F32)]
        + [tile, one, pltpu.SemaphoreType.DMA((5, PARTS))]
        + [one] * 6
        + [each] * 12
    )
    outs = pl.pallas_call(
        kernel,
        out_shape=[narrow] * 5 + [tile],
        in_specs=[any_space] * 6,
        out_specs=[vmem] * 6,
        scratch_shapes=scratch,
        compiler_params=pltpu.CompilerParams(
            collective_id=0, has_side_effects=True, vmem_limit_bytes=56 * 2**20
        ),
        name="lightning",
    )(query, key_in, value, gate, grad_out, gain.reshape(8, WIDTH))
    gated, dq, dk, dv, gg, gain_gradient = pl.pallas_call(
        store,
        out_shape=[big] * 5 + [jax.ShapeDtypeStruct((8, WIDTH), F32)],
        in_specs=[any_space] * 6,
        out_specs=[any_space] * 6,
        scratch_shapes=[pltpu.SemaphoreType.DMA((6,))],
        compiler_params=pltpu.CompilerParams(vmem_limit_bytes=4 * 2**20),
        name="store",
    )(*outs)
    return gated, dq, dk, dv, gg, gain_gradient.reshape(-1)


def solution(mesh):
    block = P("ctx", "tp")
    specs = (block, block, block, block, P("tp"), block)
    out_specs = (block, block, block, block, block, P("tp"))
    return jax.shard_map(body, mesh=mesh, in_specs=specs, out_specs=out_specs, check_vma=False)
```
